128 devices in a mesh: lon: 16 (over x, z_hi, core), lat: 4 (over y), section: 2 (over z_lo).
Axes of the slice: x: 4, y: 4, z: 4 (z_hi: 2, z_lo: 2; z = z_hi * 2 + z_lo), core: 2. Of those that a mesh axis runs over, the one named last changes fastest.
Arguments:
- residual_stream: bfloat16 [2, 4, 16, 144, 1536], P('section', 'lat', 'lon'), may hold values from -6 to 6
- grad_out: bfloat16 [2, 4, 16, 144, 1536], P('section', 'lat', 'lon'), may hold values from -6 to 6
- norm_gain: float32 [1536], replicated, may hold values from 0.5 to 1.5
- expert_ids: int32 [2, 4, 16, 144, 2], P('section', 'lat', 'lon'), may hold values from 0 to 15, all different within a row; in each aligned block of 144 rows (0 to 143, 144 to 287, ..., all dimensions but the last counted through in order) at most 27 rows name the same one
- route_weights: float32 [2, 4, 16, 144, 2], P('section', 'lat', 'lon'), may hold values from 0.1 to 0.9
- gate_saved: bfloat16 [16, 4, 2, 16, 27, 6144], P('lon', None, None, None, None, ('lat', 'section')), may hold values from -6 to 6
- up_saved: bfloat16 [16, 4, 2, 16, 27, 6144], P('lon', None, None, None, None, ('lat', 'section')), may hold values from -6 to 6
- gate_weight: bfloat16 [16, 1536, 6144], P('lon', None, ('lat', 'section')), may hold values from -0.15625 to 0.15625
- up_weight: bfloat16 [16, 1536, 6144], P('lon', None, ('lat', 'section')), may hold values from -0.15625 to 0.15625
- down_weight: bfloat16 [16, 6144, 1536], P('lon', ('lat', 'section')), may hold values from -0.078125 to 0.078125
- queries: bfloat16 [2, 4, 16, 144, 1536], P('section', 'lat', 'lon'), may hold values from -6 to 6
- key_states: bfloat16 [2, 4, 16, 144, 1536], P('section', 'lat', 'lon'), may hold values from -6 to 6
- value_states: bfloat16 [2, 4, 16, 144, 1536], P('section', 'lat', 'lon'), may hold values from -6 to 6
- window_bias: bfloat16 [4, 24, 144, 144], P('lat'), may hold values from -3 to 300
Outputs:
- grad_hidden: bfloat16 [2, 4, 16, 144, 1536], P('section', 'lat', 'lon')
- grad_queries: bfloat16 [2, 4, 16, 144, 1536], P('section', 'lat', 'lon')
- grad_keys: bfloat16 [2, 4, 16, 144, 1536], P('section', 'lat', 'lon')
- grad_values: bfloat16 [2, 4, 16, 144, 1536], P('section', 'lat', 'lon')
The draws below stay inside these ranges and needn't reach their ends.
Inputs may be any that keep to these rules, and one draw needn't show every extreme that they name: `expert_ids`: among the routes of the 144 tokens of one device no expert is named more than 27 times, a bound that some block reaches; the 2 experts of a token differ.
All inputs are finite; a program needn't handle non-finite values.
Results may differ from the reference program's by a relative error of at most 0.02.
Values may be sent and summed in bfloat16 or wider, within the bound.
No kernel may reach another device: no remote copies, remote signals or barrier semaphores. Data moves between devices by JAX's collectives and lax.ppermute only.
A program may use at most 256 MiB of HBM per device.

```python
import math
import jax
import jax.numpy as jnp
import numpy as np
from jax import lax

D = 1536
HEADS = 24
HD = 64
FF = 6144
TOP = 2
LEVELS = 2
WIN_LAT = 6
WIN_LON = 12
WL = 1
PTS = 144
TOK_DEV = 144
NWIN = 16
EXPERTS = 16
CAP = 27
N_LON = 16
N_LAT = 4
N_SECTION = 2


def draw_window_bias(key, part):
    key = jax.random.fold_in(key, 17)
    base_key = jax.random.fold_in(key, 0)
    bias_shape = (N_LAT, HEADS, PTS, PTS)
    values = jnp.clip(jax.random.normal(base_key, bias_shape, jnp.float32), -3.0, 3.0)
    return values.astype(jnp.bfloat16)


def block_scale(stream_key, extent, cuts, low, top_value):
    def one(axis_at, shards_of):
        steps = jax.random.uniform(jax.random.fold_in(jax.random.fold_in(stream_key, 6), axis_at), (shards_of,), jnp.float32, low / len(cuts), top_value / len(cuts))
        return jnp.repeat(jnp.exp(steps), extent[axis_at] // shards_of).reshape((-1,) + (1,) * (len(extent) - axis_at - 1))

    loudness = one(*cuts[0])
    for cut in cuts[1:]:
        loudness = loudness * one(*cut)
    return loudness


def routed_block(rng, own, number, rows, count, top, reach, skew):
    sequence = jax.random.permutation(rng, count)
    packed, ordinary = portions_of(count, rows * top, reach, skew, True), portions_of(count, rows * top, reach, skew, False)
    places = jnp.arange(count)

    def named(tallies, turn):
        used = int((tallies > 0).sum())
        fixed = max(1, used // 4)
        moved = fixed + (places - fixed + turn * (used - fixed)) % max(1, count - fixed)
        return jnp.zeros((count,), jnp.int32).at[sequence[jnp.where(places < fixed, places, moved)]].set(jnp.asarray(tallies, jnp.int32))

    tallies = jnp.where(number % 4 == 0, named(packed, number // 4), named(ordinary, number - number // 4 - 1))
    mixed = jax.random.permutation(jax.random.fold_in(own, 3), count)
    donor, receiver = mixed[0:count // 2 * 2:2], mixed[1:count // 2 * 2:2]
    room = jnp.minimum(tallies[donor] - 1, reach - tallies[receiver]) // 2
    room = jnp.where((donor == sequence[0]) | (receiver == sequence[0]) | (tallies[receiver] == 0), 0, jnp.maximum(room, 0))
    moved = jax.random.randint(jax.random.fold_in(own, 4), (count // 2,), 0, 1 << 20) % (room + 1)
    tallies = tallies.at[donor].add(-moved).at[receiver].add(moved)
    members = jnp.searchsorted(jnp.cumsum(tallies), jnp.arange(rows * top), side="right").astype(jnp.int32)
    table = members.reshape(top, rows).T
    table = table[jax.random.permutation(jax.random.fold_in(own, 1), rows)]
    turn = jax.random.randint(jax.random.fold_in(own, 2), (rows, 1), 0, top)
    return jnp.take_along_axis(table, (jnp.arange(top)[None, :] + turn) % top, axis=1)


def portions_of(count, total, bound, skew, full):
    weights = [(1 << 20) // math.isqrt(standing ** skew) + 1 for standing in range(1, count + 1)]
    largest = bound if full else min(bound, max(-(-total // count), total * weights[0] // sum(weights)))
    least = 1 if total - largest >= count - 1 else 0
    given, spare = [largest] + [least] * (count - 1), total - largest - least * (count - 1)
    while spare > 0:
        candidates = [i for i in range(1, count) if given[i] < largest] or [i for i in range(1, count) if given[i] < bound]
        pool, remaining = sum([weights[i] for i in candidates]), spare
        for i in candidates:
            more = min(bound - given[i], max(1, remaining * weights[i] // pool), spare)
            given[i] = given[i] + more
            spare = spare - more
    return np.array(given)


def bell_draw(rng, shape, spread, reach, shards=(), held_as=jnp.bfloat16):
    loudness = block_scale(rng, shape, shards, -0.22, 0.18) if shards else 1.0
    drawn = jax.random.normal(rng, shape, jnp.float32) * spread * loudness
    return jnp.minimum(jnp.maximum(drawn, -reach), reach).astype(held_as)


def setup_inputs(seed: int = 0) -> dict:
    arg_keys = jax.random.split(jax.random.key(seed), 15)
    residual_stream = bell_draw(arg_keys[0], (N_SECTION, N_LAT, NWIN, PTS, D), 1.0, 6.0, ((0, 2), (1, 4), (2, 16)))
    grad_out = bell_draw(arg_keys[1], (N_SECTION, N_LAT, NWIN, PTS, D), 1.0, 6.0, ((0, 2), (1, 4), (2, 16)))
    norm_gain = jnp.clip(1.0 + 0.1 * jax.random.normal(arg_keys[2], (D,), jnp.float32), 0.5, 1.5)
    expert_ids_keys = jax.random.split(jax.random.fold_in(arg_keys[3], 1), N_SECTION * N_LAT * NWIN * PTS // TOK_DEV)
    expert_ids_turns = jax.random.permutation(jax.random.fold_in(arg_keys[3], 3), N_SECTION * N_LAT * NWIN * PTS // TOK_DEV)
    expert_ids = jax.vmap(lambda own, number: routed_block(jax.random.fold_in(arg_keys[3], 2), own, number, TOK_DEV, EXPERTS, TOP, CAP, 2))(expert_ids_keys, expert_ids_turns).reshape((N_SECTION, N_LAT, NWIN, PTS, TOP))
    route_weights = jnp.clip(0.1 + 0.79999997 * jax.random.uniform(arg_keys[4], (N_SECTION, N_LAT, NWIN, PTS, TOP), jnp.float32) ** block_scale(arg_keys[4], (N_SECTION, N_LAT, NWIN, PTS, TOP), ((0, 2), (1, 4), (2, 16)), -0.2, 0.2), 0.1, 0.9)
    gate_saved = bell_draw(arg_keys[5], (EXPERTS, N_LAT, N_SECTION, N_LON, CAP, FF), 1.0, 6.0, ((0, 16), (5, 8)))
    up_saved = bell_draw(arg_keys[6], (EXPERTS, N_LAT, N_SECTION, N_LON, CAP, FF), 1.0, 6.0, ((0, 16), (5, 8)))
    gate_weight = bell_draw(arg_keys[7], (EXPERTS, D, FF), D ** -0.5, 0.15625, ((0, 16), (2, 8)))
    up_weight = bell_draw(arg_keys[8], (EXPERTS, D, FF), D ** -0.5, 0.15625, ((0, 16), (2, 8)))
    down_weight = bell_draw(arg_keys[9], (EXPERTS, FF, D), FF ** -0.5, 0.078125, ((0, 16), (1, 8)))
    queries = bell_draw(arg_keys[10], (N_SECTION, N_LAT, NWIN, PTS, D), 1.0, 6.0, ((0, 2), (1, 4), (2, 16)))
    key_states = bell_draw(arg_keys[11], (N_SECTION, N_LAT, NWIN, PTS, D), 1.0, 6.0, ((0, 2), (1, 4), (2, 16)))
    value_states = bell_draw(arg_keys[12], (N_SECTION, N_LAT, NWIN, PTS, D), 1.0, 6.0, ((0, 2), (1, 4), (2, 16)))
    window_bias = draw_window_bias(jax.random.fold_in(arg_keys[14], 71), 0)
    return dict(residual_stream=residual_stream, grad_out=grad_out, norm_gain=norm_gain, expert_ids=expert_ids, route_weights=route_weights, gate_saved=gate_saved, up_saved=up_saved, gate_weight=gate_weight, up_weight=up_weight, down_weight=down_weight, queries=queries, key_states=key_states, value_states=value_states, window_bias=window_bias)


EPSILON = 1e-06

def reference(residual_stream, grad_out, norm_gain, expert_ids, route_weights, gate_saved, up_saved, gate_weight, up_weight, down_weight, queries, key_states, value_states, window_bias):
    groups = N_LAT * N_SECTION
    shard_width = FF // groups
    dev_rows = WL * PTS
    hidden = residual_stream.astype(jnp.float32)
    upstream = grad_out.astype(jnp.float32)
    scaled = (route_weights[..., None] * upstream[..., None, :]).astype(jnp.bfloat16)
    blocks = scaled.reshape(N_SECTION, N_LAT, N_LON, dev_rows * TOP, D)
    chosen = expert_ids.reshape(N_SECTION, N_LAT, N_LON, dev_rows * TOP)
    onehot = (chosen[..., None] == jnp.arange(EXPERTS, dtype=jnp.int32)).astype(jnp.int32)
    slot_of = lax.optimization_barrier(jnp.sum((jnp.cumsum(onehot, axis=3) - onehot) * onehot, axis=-1)).astype(jnp.int32)
    section_idx = lax.broadcasted_iota(jnp.int32, chosen.shape, 0)
    lat_idx = lax.broadcasted_iota(jnp.int32, chosen.shape, 1)
    lon_idx = lax.broadcasted_iota(jnp.int32, chosen.shape, 2)
    rows_in = jnp.zeros((EXPERTS, N_LAT, N_SECTION, N_LON, CAP, D), jnp.bfloat16)
    rows_in = rows_in.at[chosen, lat_idx, section_idx, lon_idx, slot_of].set(blocks)

    def per_expert(expert):
        incoming = rows_in[expert].reshape(-1, D).astype(jnp.float32)
        gate_pre = gate_saved[expert].reshape(-1, groups, shard_width).astype(jnp.float32)
        up_pre = up_saved[expert].reshape(-1, groups, shard_width).astype(jnp.float32)
        down_mat = down_weight[expert].astype(jnp.float32).reshape(groups, shard_width, D)
        gate_mat = gate_weight[expert].astype(jnp.float32).reshape(D, groups, shard_width)
        up_mat = up_weight[expert].astype(jnp.float32).reshape(D, groups, shard_width)
        back_grad = jnp.einsum('rd,jfd->rjf', incoming, down_mat)
        sigma = jax.nn.sigmoid(gate_pre)
        d_gate = lax.optimization_barrier((back_grad * up_pre * sigma * (1.0 + gate_pre * (1.0 - sigma))).astype(jnp.bfloat16)).astype(jnp.float32)
        d_up = lax.optimization_barrier((back_grad * gate_pre * sigma).astype(jnp.bfloat16)).astype(jnp.float32)
        partial_grad = jnp.einsum('rjf,djf->jrd', d_gate, gate_mat) + jnp.einsum('rjf,djf->jrd', d_up, up_mat)
        partial_grad = lax.optimization_barrier(partial_grad.astype(jnp.bfloat16)).astype(jnp.float32)
        return lax.optimization_barrier(jnp.sum(partial_grad, axis=0)).astype(jnp.bfloat16).reshape(N_LAT, N_SECTION, N_LON, CAP, D)
    grad_rows = lax.map(per_expert, jnp.arange(EXPERTS, dtype=jnp.int32))
    per_route = grad_rows[chosen, lat_idx, section_idx, lon_idx, slot_of].astype(jnp.float32)
    grad_normed = per_route.reshape(N_SECTION, N_LAT, N_LON, dev_rows, TOP, D).sum(axis=4).reshape(hidden.shape)
    inverse = lax.rsqrt(lax.optimization_barrier(jnp.mean(hidden * hidden, axis=-1, keepdims=True)) + EPSILON)
    normed = hidden * inverse
    d_normed = grad_normed * norm_gain
    inner = lax.optimization_barrier(jnp.mean(d_normed * normed, axis=-1, keepdims=True))
    grad_hidden = (upstream + inverse * (d_normed - normed * inner)).astype(jnp.bfloat16)
    half = WIN_LON // 2
    grid = grad_hidden.reshape(N_SECTION, N_LAT, NWIN, LEVELS, WIN_LAT, WIN_LON, D)
    east_part = jnp.roll(grid[..., :half, :], -1, axis=2)
    shifted = jnp.concatenate([grid[..., half:, :], east_part], axis=5)
    context_grad = shifted.reshape(N_SECTION, N_LAT, NWIN, PTS, HEADS, HD).astype(jnp.float32)
    scale = HD ** (-0.5)
    query_f = queries.reshape(N_SECTION, N_LAT, NWIN, PTS, HEADS, HD).astype(jnp.float32)
    key_f = key_states.reshape(N_SECTION, N_LAT, NWIN, PTS, HEADS, HD).astype(jnp.float32)
    value_f = value_states.reshape(N_SECTION, N_LAT, NWIN, PTS, HEADS, HD).astype(jnp.float32)
    scores = jnp.einsum('slwqhd,slwkhd->slwhqk', query_f, key_f) * scale + window_bias.astype(jnp.float32)[None, :, None]
    probs = jax.nn.softmax(scores, axis=-1)
    probs_low = lax.optimization_barrier(probs.astype(jnp.bfloat16)).astype(jnp.float32)
    grad_probs = jnp.einsum('slwqhd,slwkhd->slwhqk', context_grad, value_f)
    delta = lax.optimization_barrier(jnp.sum(probs * grad_probs, axis=-1, keepdims=True))
    grad_scores = lax.optimization_barrier((probs * (grad_probs - delta)).astype(jnp.bfloat16)).astype(jnp.float32)
    grad_queries = (jnp.einsum('slwhqk,slwkhd->slwqhd', grad_scores, key_f) * scale).astype(jnp.bfloat16)
    grad_keys = (jnp.einsum('slwhqk,slwqhd->slwkhd', grad_scores, query_f) * scale).astype(jnp.bfloat16)
    grad_values = jnp.einsum('slwhqk,slwqhd->slwkhd', probs_low, context_grad).astype(jnp.bfloat16)
    out_shape = residual_stream.shape
    return (grad_hidden, grad_queries.reshape(out_shape), grad_keys.reshape(out_shape), grad_values.reshape(out_shape))
```

```python
import jax
import jax.numpy as jnp
from jax import lax
from jax.sharding import PartitionSpec as P

HEADS = 24
HD = 64
TOP = 2
LEVELS = 2
WIN_LAT = 6
WIN_LON = 12
FIRST_SLOTS = 15


EPSILON = 1e-06


def passed_along(x, axis, by):
    devices = lax.axis_size(axis)
    return lax.ppermute(x, axis, [(i, (i + by) % devices) for i in range(devices)])


def expert_term(incoming, gate_rows, up_rows, gate_mat, up_mat, down_mat):
    contract = (((1,), (1,)), ((), ()))
    back_grad = lax.dot_general(incoming, down_mat, contract, preferred_element_type=jnp.float32)
    gate_pre = gate_rows.astype(jnp.float32)
    up_pre = up_rows.astype(jnp.float32)
    sigma = jax.nn.sigmoid(gate_pre)
    d_gate = (back_grad * up_pre * sigma * (1.0 + gate_pre * (1.0 - sigma))).astype(jnp.bfloat16)
    d_up = (back_grad * gate_pre * sigma).astype(jnp.bfloat16)
    total = lax.dot_general(d_gate, gate_mat, contract, preferred_element_type=jnp.float32)
    return total + lax.dot_general(d_up, up_mat, contract, preferred_element_type=jnp.float32)


def per_device(
    residual_stream,
    grad_out,
    norm_gain,
    expert_ids,
    route_weights,
    gate_saved,
    up_saved,
    gate_weight,
    up_weight,
    down_weight,
    queries,
    key_states,
    value_states,
    window_bias,
):
    lon_count = lax.axis_size("lon")
    lat_count = lax.axis_size("lat")
    section_count = lax.axis_size("section")
    windows = residual_stream.shape[2]
    points = residual_stream.shape[3]
    width = residual_stream.shape[4]
    tok_rows = windows * points
    capacity = gate_saved.shape[4]
    shard_width = gate_saved.shape[5]
    route_count = tok_rows * TOP
    hidden = residual_stream.reshape(tok_rows, width).astype(jnp.float32)
    upstream = grad_out.reshape(tok_rows, width)
    chosen = expert_ids.reshape(route_count)
    weights = route_weights.reshape(tok_rows, TOP)
    scaled = (
        (weights[:, :, None] * upstream[:, None, :].astype(jnp.float32))
        .astype(jnp.bfloat16)
        .reshape(route_count, width)
    )
    onehot = (chosen[:, None] == jnp.arange(lon_count, dtype=jnp.int32)[None, :]).astype(jnp.int32)
    slot_of = jnp.sum((jnp.cumsum(onehot, axis=0) - onehot) * onehot, axis=1)
    target = chosen * capacity + slot_of
    placing = (
        target[None, :] == jnp.arange(lon_count * capacity, dtype=jnp.int32)[:, None]
    ).astype(jnp.bfloat16)
    outgoing = (
        jnp.dot(placing, scaled, preferred_element_type=jnp.float32)
        .astype(jnp.bfloat16)
        .reshape(lon_count, capacity, width)
    )
    gate_mat = gate_weight[0]
    up_mat = up_weight[0]
    down_mat = down_weight[0]
    arrived = lax.all_to_all(outgoing, "lon", split_axis=0, concat_axis=0, tiled=True)
    arrived = arrived.transpose(1, 0, 2).reshape(lon_count * capacity, width)
    gate_flat = gate_saved[0].transpose(0, 1, 3, 2, 4).reshape(
        lat_count, section_count, lon_count * capacity, shard_width
    )
    up_flat = up_saved[0].transpose(0, 1, 3, 2, 4).reshape(
        lat_count, section_count, lon_count * capacity, shard_width
    )
    lat = lax.axis_index("lat")
    section = lax.axis_index("section")
    first = FIRST_SLOTS * lon_count

    def term(incoming, lat_step, section_step, low, high):
        at = (lax.rem(lat - lat_step + lat_count, lat_count), section ^ section_step, low, 0)
        size = (1, 1, high - low, shard_width)
        gate_rows = lax.dynamic_slice(gate_flat, at, size)[0, 0]
        up_rows = lax.dynamic_slice(up_flat, at, size)[0, 0]
        return expert_term(incoming, gate_rows, up_rows, gate_mat, up_mat, down_mat)

    steps = (1, -1, 2)
    high_rows = {(0, 0): arrived[:first]}
    low_rows = {(0, 0): arrived[first:]}
    high_rows[0, 1] = passed_along(high_rows[0, 0], "section", 1)
    for step in steps:
        low_rows[step, 0] = passed_along(low_rows[0, 0], "lat", step)
    low_rows[0, 1] = passed_along(low_rows[0, 0], "section", 1)
    for step in steps:
        high_rows[step, 0] = passed_along(high_rows[0, 0], "lat", step)
    for step in steps:
        low_rows[step, 1] = passed_along(low_rows[step, 0], "section", 1)
        high_rows[step, 1] = passed_along(high_rows[0, 1], "lat", step)

    high_term = {}
    low_term = {}
    for side in (0, 1):
        for step in (0,) + steps:
            low_term[step, side] = term(
                low_rows[step, side], step, side, first, lon_count * capacity
            )
    for side in (0, 1):
        for step in (0,) + steps:
            high_term[step, side] = term(high_rows[step, side], step, side, 0, first)

    low_sum = {}
    for step in (0,) + steps:
        sent = passed_along(low_term[step, 1].astype(jnp.bfloat16), "section", 1)
        low_sum[step] = low_term[step, 0] + sent.astype(jnp.float32)
    low_total = low_sum[0]
    for step in steps:
        sent = passed_along(low_sum[step].astype(jnp.bfloat16), "lat", -step)
        low_total = low_total + sent.astype(jnp.float32)
    high_sum = {}
    for side in (1, 0):
        total = high_term[0, side]
        for step in steps:
            sent = passed_along(high_term[step, side].astype(jnp.bfloat16), "lat", -step)
            total = total + sent.astype(jnp.float32)
        high_sum[side] = total
    sent = passed_along(high_sum[1].astype(jnp.bfloat16), "section", 1)
    high_total = high_sum[0] + sent.astype(jnp.float32)
    summed = jnp.concatenate([high_total, low_total], axis=0).astype(jnp.bfloat16)
    returned = summed.reshape(capacity, lon_count, width).transpose(1, 0, 2)
    back_rows = lax.all_to_all(returned, "lon", split_axis=0, concat_axis=0, tiled=True)
    combine = (
        placing.reshape(lon_count * capacity, tok_rows, TOP)
        .astype(jnp.float32)
        .sum(axis=2)
        .astype(jnp.bfloat16)
    )
    grad_normed = lax.dot_general(
        combine,
        back_rows.reshape(lon_count * capacity, width),
        (((0,), (0,)), ((), ())),
        preferred_element_type=jnp.float32,
    )
    inverse = lax.rsqrt(jnp.mean(hidden * hidden, axis=-1, keepdims=True) + EPSILON)
    normed = hidden * inverse
    d_normed = grad_normed * norm_gain
    inner = jnp.mean(d_normed * normed, axis=-1, keepdims=True)
    grad_hidden = (upstream.astype(jnp.float32) + inverse * (d_normed - normed * inner)).astype(
        jnp.bfloat16
    )
    half = WIN_LON // 2
    grid = grad_hidden.reshape(windows, LEVELS, WIN_LAT, WIN_LON, width)
    western = passed_along(grid[0:1, :, :, :half, :], "lon", -1)
    east_part = jnp.concatenate([grid[1:, :, :, :half, :], western], axis=0)
    context_grad = jnp.concatenate([grid[:, :, :, half:, :], east_part], axis=3).reshape(
        windows, points, HEADS, HD
    )
    scale = HD ** (-0.5)
    query_part = queries.reshape(windows, points, HEADS, HD)
    key_part = key_states.reshape(windows, points, HEADS, HD)
    value_part = value_states.reshape(windows, points, HEADS, HD)
    scores = (
        jnp.einsum("wqhd,wkhd->whqk", query_part, key_part, preferred_element_type=jnp.float32)
        * scale
    )
    scores = scores + window_bias[0].astype(jnp.float32)[None]
    probs = jax.nn.softmax(scores, axis=-1)
    probs_low = probs.astype(jnp.bfloat16)
    grad_probs = jnp.einsum(
        "wqhd,wkhd->whqk", context_grad, value_part, preferred_element_type=jnp.float32
    )
    delta = jnp.sum(probs * grad_probs, axis=-1, keepdims=True)
    grad_scores = (probs * (grad_probs - delta)).astype(jnp.bfloat16)
    grad_queries = (
        jnp.einsum("whqk,wkhd->wqhd", grad_scores, key_part, preferred_element_type=jnp.float32)
        * scale
    ).astype(jnp.bfloat16)
    grad_keys = (
        jnp.einsum("whqk,wqhd->wkhd", grad_scores, query_part, preferred_element_type=jnp.float32)
        * scale
    ).astype(jnp.bfloat16)
    grad_values = jnp.einsum(
        "whqk,wqhd->wkhd", probs_low, context_grad, preferred_element_type=jnp.float32
    ).astype(jnp.bfloat16)
    out_shape = residual_stream.shape
    return (
        grad_hidden.reshape(out_shape),
        grad_queries.reshape(out_shape),
        grad_keys.reshape(out_shape),
        grad_values.reshape(out_shape),
    )


def solution(mesh):
    placed = (
        P("section", "lat", "lon", None, None),
        P("section", "lat", "lon", None, None),
        P(),
        P("section", "lat", "lon", None, None),
        P("section", "lat", "lon", None, None),
        P("lon", None, None, None, None, ("lat", "section")),
        P("lon", None, None, None, None, ("lat", "section")),
        P("lon", None, ("lat", "section")),
        P("lon", None, ("lat", "section")),
        P("lon", ("lat", "section"), None),
        P("section", "lat", "lon", None, None),
        P("section", "lat", "lon", None, None),
        P("section", "lat", "lon", None, None),
        P("lat", None, None, None),
    )
    return jax.shard_map(
        per_device,
        mesh=mesh,
        in_specs=placed,
        out_specs=(
            P("section", "lat", "lon", None, None),
            P("section", "lat", "lon", None, None),
            P("section", "lat", "lon", None, None),
            P("section", "lat", "lon", None, None),
        ),
        check_vma=False,
    )
```

```python
import jax
import jax.numpy as jnp
from jax import lax
from jax.sharding import PartitionSpec as P

HEADS = 24
HD = 64
TOP = 2
LEVELS = 2
WIN_LAT = 6
WIN_LON = 12
FIRST_SLOTS = 16


EPSILON = 1e-06


def passed_along(x, axis, by):
    devices = lax.axis_size(axis)
    return lax.ppermute(x, axis, [(i, (i + by) % devices) for i in range(devices)])


def expert_term(incoming, gate_rows, up_rows, gate_mat, up_mat, down_mat):
    contract = (((1,), (1,)), ((), ()))
    back_grad = lax.dot_general(incoming, down_mat, contract, preferred_element_type=jnp.float32)
    gate_pre = gate_rows.astype(jnp.float32)
    up_pre = up_rows.astype(jnp.float32)
    sigma = jax.nn.sigmoid(gate_pre)
    d_gate = (back_grad * up_pre * sigma * (1.0 + gate_pre * (1.0 - sigma))).astype(jnp.bfloat16)
    d_up = (back_grad * gate_pre * sigma).astype(jnp.bfloat16)
    total = lax.dot_general(d_gate, gate_mat, contract, preferred_element_type=jnp.float32)
    return total + lax.dot_general(d_up, up_mat, contract, preferred_element_type=jnp.float32)


def per_device(
    residual_stream,
    grad_out,
    norm_gain,
    expert_ids,
    route_weights,
    gate_saved,
    up_saved,
    gate_weight,
    up_weight,
    down_weight,
    queries,
    key_states,
    value_states,
    window_bias,
):
    lon_count = lax.axis_size("lon")
    lat_count = lax.axis_size("lat")
    section_count = lax.axis_size("section")
    windows = residual_stream.shape[2]
    points = residual_stream.shape[3]
    width = residual_stream.shape[4]
    tok_rows = windows * points
    capacity = gate_saved.shape[4]
    shard_width = gate_saved.shape[5]
    route_count = tok_rows * TOP
    hidden = residual_stream.reshape(tok_rows, width).astype(jnp.float32)
    upstream = grad_out.reshape(tok_rows, width)
    chosen = expert_ids.reshape(route_count)
    weights = route_weights.reshape(tok_rows, TOP)
    scaled = (
        (weights[:, :, None] * upstream[:, None, :].astype(jnp.float32))
        .astype(jnp.bfloat16)
        .reshape(route_count, width)
    )
    onehot = (chosen[:, None] == jnp.arange(lon_count, dtype=jnp.int32)[None, :]).astype(jnp.int32)
    slot_of = jnp.sum((jnp.cumsum(onehot, axis=0) - onehot) * onehot, axis=1)
    target = chosen * capacity + slot_of
    placing = (
        target[None, :] == jnp.arange(lon_count * capacity, dtype=jnp.int32)[:, None]
    ).astype(jnp.bfloat16)
    outgoing = (
        jnp.dot(placing, scaled, preferred_element_type=jnp.float32)
        .astype(jnp.bfloat16)
        .reshape(lon_count, capacity, width)
    )
    gate_mat = gate_weight[0]
    up_mat = up_weight[0]
    down_mat = down_weight[0]
    arrived = lax.all_to_all(outgoing, "lon", split_axis=0, concat_axis=0, tiled=True)
    arrived = arrived.transpose(1, 0, 2).reshape(lon_count * capacity, width)
    gate_flat = gate_saved[0].transpose(0, 1, 3, 2, 4).reshape(
        lat_count, section_count, lon_count * capacity, shard_width
    )
    up_flat = up_saved[0].transpose(0, 1, 3, 2, 4).reshape(
        lat_count, section_count, lon_count * capacity, shard_width
    )
    lat = lax.axis_index("lat")
    section = lax.axis_index("section")
    first = FIRST_SLOTS * lon_count

    def term(incoming, lat_step, section_step, low, high):
        at = (lax.rem(lat - lat_step + lat_count, lat_count), section ^ section_step, low, 0)
        size = (1, 1, high - low, shard_width)
        gate_rows = lax.dynamic_slice(gate_flat, at, size)[0, 0]
        up_rows = lax.dynamic_slice(up_flat, at, size)[0, 0]
        return expert_term(incoming, gate_rows, up_rows, gate_mat, up_mat, down_mat)

    count = lon_count * capacity
    half = count // 2
    half_high = first // 2
    landed = []

    def start(x, way):
        if landed:
            x = lax.optimization_barrier((x,) + tuple(landed))[0]
        if way:
            return passed_along(x, "lat", way)
        return passed_along(x, "section", 1)

    def both_ways(up, down):
        return start(up, 1), start(down, -1)

    def land(*arrays):
        landed.extend(arrays)
        del landed[:-4]

    def rounded(x):
        return x.astype(jnp.bfloat16)

    def widened(x):
        return x.astype(jnp.float32)

    def low_term(rows, step, side):
        return term(rows, step, side, first, count)

    def high_term(rows, step, side):
        return term(rows, step, side, 0, first)

    def far_back(x, cut):
        x = rounded(x)
        return both_ways(x[cut:], x[:cut])

    def near_back(up, down, got, cut):
        from_down, from_up = got
        up = jnp.concatenate([up[:cut] + widened(from_up), up[cut:]], axis=0)
        down = jnp.concatenate([down[:cut], down[cut:] + widened(from_down)], axis=0)
        return both_ways(rounded(down), rounded(up))

    def summed_up(own, got):
        return own + widened(got[0]) + widened(got[1])

    high = arrived[:first]
    low = arrived[first:]
    up, down = both_ways(arrived, arrived)
    high_z = start(high, 0)
    land(high_z)
    low_z = start(low, 0)
    land(up, down)
    far = both_ways(up[:half], down[half:])
    high_up_z, high_down_z = both_ways(high_z, high_z)
    land(low_z)
    low_up_z = start(up[first:], 0)
    land(low_up_z)
    low_down_z = start(down[first:], 0)
    land(*far)
    far = jnp.concatenate(far, axis=0)
    land(low_down_z)
    low_far_z = start(far[first:], 0)
    land(high_up_z, high_down_z)
    far_z = both_ways(high_up_z[:half_high], high_down_z[half_high:])
    land(*far_z)
    high_far_z = jnp.concatenate(far_z, axis=0)
    far_1 = far_back(high_term(high_far_z, 2, 1), half_high)
    land(low_far_z)
    crossed_far = start(rounded(low_term(low_far_z, 2, 1)), 0)
    land(*far_1)
    near_1 = near_back(
        high_term(high_up_z, 1, 1), high_term(high_down_z, -1, 1), far_1, half_high
    )
    land(crossed_far)
    crossed_up = start(rounded(low_term(low_up_z, 1, 1)), 0)
    far_0 = far_back(
        jnp.concatenate(
            [
                high_term(far[:first], 2, 0),
                low_term(far[first:], 2, 0) + widened(crossed_far),
            ],
            axis=0,
        ),
        half,
    )
    land(crossed_up)
    crossed_down = start(rounded(low_term(low_down_z, -1, 1)), 0)
    land(*near_1)
    land(*far_0)
    land(crossed_down)
    near_0 = near_back(
        jnp.concatenate(
            [
                high_term(up[:first], 1, 0),
                low_term(up[first:], 1, 0) + widened(crossed_up),
            ],
            axis=0,
        ),
        jnp.concatenate(
            [
                high_term(down[:first], -1, 0),
                low_term(down[first:], -1, 0) + widened(crossed_down),
            ],
            axis=0,
        ),
        far_0,
        half,
    )
    crossed_high = start(rounded(summed_up(high_term(high_z, 0, 1), near_1)), 0)
    land(crossed_high)
    crossed_low = start(rounded(low_term(low_z, 0, 1)), 0)
    crossed = jnp.concatenate([crossed_high, crossed_low], axis=0)
    own = jnp.concatenate([high_term(high, 0, 0), low_term(low, 0, 0)], axis=0)
    summed = rounded(summed_up(own + widened(crossed), near_0))
    returned = summed.reshape(capacity, lon_count, width).transpose(1, 0, 2)
    back_rows = lax.all_to_all(returned, "lon", split_axis=0, concat_axis=0, tiled=True)
    combine = (
        placing.reshape(lon_count * capacity, tok_rows, TOP)
        .astype(jnp.float32)
        .sum(axis=2)
        .astype(jnp.bfloat16)
    )
    grad_normed = lax.dot_general(
        combine,
        back_rows.reshape(lon_count * capacity, width),
        (((0,), (0,)), ((), ())),
        preferred_element_type=jnp.float32,
    )
    inverse = lax.rsqrt(jnp.mean(hidden * hidden, axis=-1, keepdims=True) + EPSILON)
    normed = hidden * inverse
    d_normed = grad_normed * norm_gain
    inner = jnp.mean(d_normed * normed, axis=-1, keepdims=True)
    grad_hidden = (upstream.astype(jnp.float32) + inverse * (d_normed - normed * inner)).astype(
        jnp.bfloat16
    )
    half = WIN_LON // 2
    grid = grad_hidden.reshape(windows, LEVELS, WIN_LAT, WIN_LON, width)
    western = passed_along(grid[0:1, :, :, :half, :], "lon", -1)
    east_part = jnp.concatenate([grid[1:, :, :, :half, :], western], axis=0)
    context_grad = jnp.concatenate([grid[:, :, :, half:, :], east_part], axis=3).reshape(
        windows, points, HEADS, HD
    )
    scale = HD ** (-0.5)
    query_part = queries.reshape(windows, points, HEADS, HD)
    key_part = key_states.reshape(windows, points, HEADS, HD)
    value_part = value_states.reshape(windows, points, HEADS, HD)
    scores = (
        jnp.einsum("wqhd,wkhd->whqk", query_part, key_part, preferred_element_type=jnp.float32)
        * scale
    )
    scores = scores + window_bias[0].astype(jnp.float32)[None]
    probs = jax.nn.softmax(scores, axis=-1)
    probs_low = probs.astype(jnp.bfloat16)
    grad_probs = jnp.einsum(
        "wqhd,wkhd->whqk", context_grad, value_part, preferred_element_type=jnp.float32
    )
    delta = jnp.sum(probs * grad_probs, axis=-1, keepdims=True)
    grad_scores = (probs * (grad_probs - delta)).astype(jnp.bfloat16)
    grad_queries = (
        jnp.einsum("whqk,wkhd->wqhd", grad_scores, key_part, preferred_element_type=jnp.float32)
        * scale
    ).astype(jnp.bfloat16)
    grad_keys = (
        jnp.einsum("whqk,wqhd->wkhd", grad_scores, query_part, preferred_element_type=jnp.float32)
        * scale
    ).astype(jnp.bfloat16)
    grad_values = jnp.einsum(
        "whqk,wqhd->wkhd", probs_low, context_grad, preferred_element_type=jnp.float32
    ).astype(jnp.bfloat16)
    out_shape = residual_stream.shape
    return (
        grad_hidden.reshape(out_shape),
        grad_queries.reshape(out_shape),
        grad_keys.reshape(out_shape),
        grad_values.reshape(out_shape),
    )


def solution(mesh):
    placed = (
        P("section", "lat", "lon", None, None),
        P("section", "lat", "lon", None, None),
        P(),
        P("section", "lat", "lon", None, None),
        P("section", "lat", "lon", None, None),
        P("lon", None, None, None, None, ("lat", "section")),
        P("lon", None, None, None, None, ("lat", "section")),
        P("lon", None, ("lat", "section")),
        P("lon", None, ("lat", "section")),
        P("lon", ("lat", "section"), None),
        P("section", "lat", "lon", None, None),
        P("section", "lat", "lon", None, None),
        P("section", "lat", "lon", None, None),
        P("lat", None, None, None),
    )
    return jax.shard_map(
        per_device,
        mesh=mesh,
        in_specs=placed,
        out_specs=(
            P("section", "lat", "lon", None, None),
            P("section", "lat", "lon", None, None),
            P("section", "lat", "lon", None, None),
            P("section", "lat", "lon", None, None),
        ),
        check_vma=False,
    )
```

```python
import jax
import jax.numpy as jnp
import numpy as np
from jax import lax
from jax.experimental import pallas as pl
from jax.experimental.pallas import tpu as pltpu
from jax.sharding import PartitionSpec as P

HEADS = 24
HD = 64
TOP = 2
WIN_LON = 12
FIRST_SLOTS = 16


EPSILON = 1e-06

LANES = 2 * HD
PAIRS_AT_ONCE = 4


def split_heads(x):
    lane = lax.broadcasted_iota(jnp.int32, x.shape, 1)
    zero = jnp.zeros_like(x)
    return jnp.concatenate([jnp.where(lane < HD, x, zero), jnp.where(lane < HD, zero, x)], axis=0)


def probs_kernel(query_ref, key_ref, bias_ref, probs_ref):
    scores = lax.dot_general(
        key_ref[...],
        split_heads(query_ref[...]),
        (((1,), (1,)), ((), ())),
        preferred_element_type=jnp.float32,
    ) * (HD ** (-0.5))
    bias = jnp.concatenate([bias_ref[0].astype(jnp.float32).T, bias_ref[1].astype(jnp.float32).T], axis=1)
    scores = scores + bias
    weight = jnp.exp(scores - jnp.max(scores, axis=0, keepdims=True))
    probs_ref[0] = weight / jnp.sum(weight, axis=0, keepdims=True)


def probabilities(query, key, bias):
    points, width = query.shape
    pairs = width // LANES
    return pl.pallas_call(
        probs_kernel,
        grid=(pairs,),
        in_specs=[
            pl.BlockSpec((points, LANES), lambda i: (0, i)),
            pl.BlockSpec((points, LANES), lambda i: (0, i)),
            pl.BlockSpec((2, points, points), lambda i: (i, 0, 0)),
        ],
        out_specs=pl.BlockSpec((1, points, 2 * points), lambda i: (i, 0, 0)),
        out_shape=jax.ShapeDtypeStruct((pairs, points, 2 * points), jnp.float32),
        cost_estimate=pl.CostEstimate(flops=2 * 10**8, bytes_accessed=4 * 10**6, transcendentals=10**6),
    )(query, key, bias)


def attention_kernel(
    own_ref, west_ref, take_own_ref, take_west_ref, query_ref, key_ref, value_ref, probs_ref,
    d_query_ref, d_key_ref, d_value_ref,
):
    context = jnp.dot(take_own_ref[...], own_ref[...], preferred_element_type=jnp.float32)
    context = context + jnp.dot(take_west_ref[...], west_ref[...], preferred_element_type=jnp.float32)
    context = context.astype(jnp.bfloat16)
    scale = HD ** (-0.5)
    points = own_ref.shape[0]
    for pair in range(PAIRS_AT_ONCE):
        at = slice(pair * LANES, (pair + 1) * LANES)
        grads = split_heads(context[:, at])
        key = key_ref[:, at]
        probs = probs_ref[pair]
        d_probs = lax.dot_general(
            value_ref[:, at], grads, (((1,), (1,)), ((), ())), preferred_element_type=jnp.float32
        )
        delta = jnp.sum(probs * d_probs, axis=0, keepdims=True)
        d_scores = (probs * (d_probs - delta)).astype(jnp.bfloat16)
        d_value_ref[:, at] = jnp.dot(
            probs.astype(jnp.bfloat16), grads, preferred_element_type=jnp.float32
        ).astype(jnp.bfloat16)
        d_key_ref[:, at] = (
            jnp.dot(d_scores, split_heads(query_ref[:, at]), preferred_element_type=jnp.float32)
            * scale
        ).astype(jnp.bfloat16)
        both = lax.dot_general(
            d_scores, key, (((0,), (0,)), ((), ())), preferred_element_type=jnp.float32
        )
        lane = lax.broadcasted_iota(jnp.int32, (points, LANES), 1)
        d_query_ref[:, at] = (jnp.where(lane < HD, both[:points], both[points:]) * scale).astype(
            jnp.bfloat16
        )


def attention_grads(own, west, query, key, value, probs):
    points, width = query.shape
    half = WIN_LON // 2
    cell = np.arange(points)
    row, column = cell // WIN_LON, cell % WIN_LON
    take_own = (column < half)[:, None] & (cell[:, None] + half == cell[None, :])
    place = row * half + column - half
    take_west = (column >= half)[:, None] & (place[:, None] == np.arange(points // 2)[None, :])
    take_own = jnp.asarray(take_own, jnp.bfloat16)
    take_west = jnp.asarray(take_west, jnp.bfloat16)
    block = PAIRS_AT_ONCE * LANES
    columns = pl.BlockSpec((points, block), lambda i: (0, i))
    return pl.pallas_call(
        attention_kernel,
        grid=(width // block,),
        in_specs=[
            columns,
            pl.BlockSpec((points // 2, block), lambda i: (0, i)),
            pl.BlockSpec(take_own.shape, lambda i: (0, 0)),
            pl.BlockSpec(take_west.shape, lambda i: (0, 0)),
            columns,
            columns,
            columns,
            pl.BlockSpec((PAIRS_AT_ONCE, points, 2 * points), lambda i: (i, 0, 0)),
        ],
        out_specs=[columns] * 3,
        out_shape=[jax.ShapeDtypeStruct((points, width), jnp.bfloat16)] * 3,
        cost_estimate=pl.CostEstimate(flops=5 * 10**8, bytes_accessed=6 * 10**6, transcendentals=0),
    )(own, west, take_own, take_west, query, key, value, probs)


def norm_kernel(
    combine_ref, back_ref, hidden_ref, upstream_ref, gain_ref, take_ref, grad_ref, west_ref
):
    grad_normed = jnp.dot(combine_ref[...], back_ref[...], preferred_element_type=jnp.float32)
    hidden = hidden_ref[...].astype(jnp.float32)
    inverse = lax.rsqrt(jnp.mean(hidden * hidden, axis=-1, keepdims=True) + EPSILON)
    normed = hidden * inverse
    d_normed = grad_normed * gain_ref[...]
    inner = jnp.mean(d_normed * normed, axis=-1, keepdims=True)
    grad = (
        upstream_ref[...].astype(jnp.float32) + inverse * (d_normed - normed * inner)
    ).astype(jnp.bfloat16)
    grad_ref[...] = grad
    west_ref[...] = jnp.dot(
        take_ref[...], grad, preferred_element_type=jnp.float32
    ).astype(jnp.bfloat16)


def norm_grads(combine, back, hidden, upstream, gain):
    points, width = hidden.shape
    half = WIN_LON // 2
    kept = np.arange(points // 2)
    take = (kept // half * WIN_LON + kept % half)[:, None] == np.arange(points)[None, :]
    return pl.pallas_call(
        norm_kernel,
        out_shape=[
            jax.ShapeDtypeStruct((points, width), jnp.bfloat16),
            jax.ShapeDtypeStruct((points // 2, width), jnp.bfloat16),
        ],
        compiler_params=pltpu.CompilerParams(vmem_limit_bytes=32 * 2**20),
        cost_estimate=pl.CostEstimate(flops=3 * 10**8, bytes_accessed=4 * 10**6, transcendentals=0),
    )(combine, back, hidden, upstream, gain.reshape(1, width), jnp.asarray(take, jnp.bfloat16))


def passed_along(x, axis, by):
    devices = lax.axis_size(axis)
    return lax.ppermute(x, axis, [(i, (i + by) % devices) for i in range(devices)])


def expert_term(incoming, gate_rows, up_rows, gate_mat, up_mat, down_mat):
    contract = (((1,), (1,)), ((), ()))
    back_grad = lax.dot_general(incoming, down_mat, contract, preferred_element_type=jnp.float32)
    gate_pre = gate_rows.astype(jnp.float32)
    up_pre = up_rows.astype(jnp.float32)
    sigma = jax.nn.sigmoid(gate_pre)
    d_gate = (back_grad * up_pre * sigma * (1.0 + gate_pre * (1.0 - sigma))).astype(jnp.bfloat16)
    d_up = (back_grad * gate_pre * sigma).astype(jnp.bfloat16)
    total = lax.dot_general(d_gate, gate_mat, contract, preferred_element_type=jnp.float32)
    return total + lax.dot_general(d_up, up_mat, contract, preferred_element_type=jnp.float32)


def per_device(
    residual_stream,
    grad_out,
    norm_gain,
    expert_ids,
    route_weights,
    gate_saved,
    up_saved,
    gate_weight,
    up_weight,
    down_weight,
    queries,
    key_states,
    value_states,
    window_bias,
):
    lon_count = lax.axis_size("lon")
    lat_count = lax.axis_size("lat")
    section_count = lax.axis_size("section")
    windows = residual_stream.shape[2]
    points = residual_stream.shape[3]
    width = residual_stream.shape[4]
    tok_rows = windows * points
    capacity = gate_saved.shape[4]
    shard_width = gate_saved.shape[5]
    route_count = tok_rows * TOP
    upstream = grad_out.reshape(tok_rows, width)
    chosen = expert_ids.reshape(route_count)
    weights = route_weights.reshape(tok_rows, TOP)
    scaled = (
        (weights[:, :, None] * upstream[:, None, :].astype(jnp.float32))
        .astype(jnp.bfloat16)
        .reshape(route_count, width)
    )
    onehot = (chosen[:, None] == jnp.arange(lon_count, dtype=jnp.int32)[None, :]).astype(jnp.int32)
    slot_of = jnp.sum((jnp.cumsum(onehot, axis=0) - onehot) * onehot, axis=1)
    target = chosen * capacity + slot_of
    placing = (
        target[None, :] == jnp.arange(lon_count * capacity, dtype=jnp.int32)[:, None]
    ).astype(jnp.bfloat16)
    outgoing = (
        jnp.dot(placing, scaled, preferred_element_type=jnp.float32)
        .astype(jnp.bfloat16)
        .reshape(lon_count, capacity, width)
    )
    gate_mat = gate_weight[0]
    up_mat = up_weight[0]
    down_mat = down_weight[0]
    arrived = lax.all_to_all(outgoing, "lon", split_axis=0, concat_axis=0, tiled=True)
    arrived = arrived.transpose(1, 0, 2).reshape(lon_count * capacity, width)
    gate_flat = gate_saved[0].transpose(0, 1, 3, 2, 4).reshape(
        lat_count, section_count, lon_count * capacity, shard_width
    )
    up_flat = up_saved[0].transpose(0, 1, 3, 2, 4).reshape(
        lat_count, section_count, lon_count * capacity, shard_width
    )
    lat = lax.axis_index("lat")
    section = lax.axis_index("section")
    first = FIRST_SLOTS * lon_count

    def term(incoming, lat_step, section_step, low, high):
        at = (lax.rem(lat - lat_step + lat_count, lat_count), section ^ section_step, low, 0)
        size = (1, 1, high - low, shard_width)
        gate_rows = lax.dynamic_slice(gate_flat, at, size)[0, 0]
        up_rows = lax.dynamic_slice(up_flat, at, size)[0, 0]
        return expert_term(incoming, gate_rows, up_rows, gate_mat, up_mat, down_mat)

    count = lon_count * capacity
    half = count // 2
    half_high = first // 2
    landed = []

    def start(x, way):
        if landed:
            x = lax.optimization_barrier((x,) + tuple(landed))[0]
        if way:
            return passed_along(x, "lat", way)
        return passed_along(x, "section", 1)

    def both_ways(up, down):
        return start(up, 1), start(down, -1)

    def land(*arrays):
        landed.extend(arrays)
        del landed[:-4]

    def rounded(x):
        return x.astype(jnp.bfloat16)

    def widened(x):
        return x.astype(jnp.float32)

    def low_term(rows, step, side):
        return term(rows, step, side, first, count)

    def high_term(rows, step, side):
        return term(rows, step, side, 0, first)

    def far_back(x, cut):
        x = rounded(x)
        return both_ways(x[cut:], x[:cut])

    def near_back(up, down, got, cut):
        from_down, from_up = got
        up = jnp.concatenate([up[:cut] + widened(from_up), up[cut:]], axis=0)
        down = jnp.concatenate([down[:cut], down[cut:] + widened(from_down)], axis=0)
        return both_ways(rounded(down), rounded(up))

    def summed_up(own, got):
        return own + widened(got[0]) + widened(got[1])

    high = arrived[:first]
    low = arrived[first:]
    up, down = both_ways(arrived, arrived)
    query = queries.reshape(points, width)
    key = key_states.reshape(points, width)
    probs = probabilities(query, key, window_bias[0])
    high_z = start(high, 0)
    land(high_z, probs)
    low_z = start(low, 0)
    land(up, down)
    far = both_ways(up[:half], down[half:])
    high_up_z, high_down_z = both_ways(high_z, high_z)
    land(low_z)
    low_up_z = start(up[first:], 0)
    land(low_up_z)
    low_down_z = start(down[first:], 0)
    land(*far)
    far = jnp.concatenate(far, axis=0)
    land(low_down_z)
    low_far_z = start(far[first:], 0)
    land(high_up_z, high_down_z)
    far_z = both_ways(high_up_z[:half_high], high_down_z[half_high:])
    land(*far_z)
    high_far_z = jnp.concatenate(far_z, axis=0)
    far_1 = far_back(high_term(high_far_z, 2, 1), half_high)
    land(low_far_z)
    crossed_far = start(rounded(low_term(low_far_z, 2, 1)), 0)
    land(*far_1)
    near_1 = near_back(
        high_term(high_up_z, 1, 1), high_term(high_down_z, -1, 1), far_1, half_high
    )
    land(crossed_far)
    crossed_up = start(rounded(low_term(low_up_z, 1, 1)), 0)
    far_0 = far_back(
        jnp.concatenate(
            [
                high_term(far[:first], 2, 0),
                low_term(far[first:], 2, 0) + widened(crossed_far),
            ],
            axis=0,
        ),
        half,
    )
    land(crossed_up)
    crossed_down = start(rounded(low_term(low_down_z, -1, 1)), 0)
    land(*near_1)
    land(*far_0)
    land(crossed_down)
    near_0 = near_back(
        jnp.concatenate(
            [
                high_term(up[:first], 1, 0),
                low_term(up[first:], 1, 0) + widened(crossed_up),
            ],
            axis=0,
        ),
        jnp.concatenate(
            [
                high_term(down[:first], -1, 0),
                low_term(down[first:], -1, 0) + widened(crossed_down),
            ],
            axis=0,
        ),
        far_0,
        half,
    )
    crossed_high = start(rounded(summed_up(high_term(high_z, 0, 1), near_1)), 0)
    land(crossed_high)
    crossed_low = start(rounded(low_term(low_z, 0, 1)), 0)
    crossed = jnp.concatenate([crossed_high, crossed_low], axis=0)
    own = jnp.concatenate([high_term(high, 0, 0), low_term(low, 0, 0)], axis=0)
    summed = rounded(summed_up(own + widened(crossed), near_0))
    returned = summed.reshape(capacity, lon_count, width).transpose(1, 0, 2)
    back_rows = lax.all_to_all(returned, "lon", split_axis=0, concat_axis=0, tiled=True)
    combine = (
        (target.reshape(tok_rows, TOP, 1) == jnp.arange(lon_count * capacity, dtype=jnp.int32))
        .any(axis=1)
        .astype(jnp.bfloat16)
    )
    grad_hidden, west = norm_grads(
        combine,
        back_rows.reshape(lon_count * capacity, width),
        residual_stream.reshape(points, width),
        upstream,
        norm_gain,
    )
    west = passed_along(west, "lon", -1)
    grad_queries, grad_keys, grad_values = attention_grads(
        grad_hidden, west, query, key, value_states.reshape(points, width), probs
    )
    out_shape = residual_stream.shape
    return (
        grad_hidden.reshape(out_shape),
        grad_queries.reshape(out_shape),
        grad_keys.reshape(out_shape),
        grad_values.reshape(out_shape),
    )


def solution(mesh):
    placed = (
        P("section", "lat", "lon", None, None),
        P("section", "lat", "lon", None, None),
        P(),
        P("section", "lat", "lon", None, None),
        P("section", "lat", "lon", None, None),
        P("lon", None, None, None, None, ("lat", "section")),
        P("lon", None, None, None, None, ("lat", "section")),
        P("lon", None, ("lat", "section")),
        P("lon", None, ("lat", "section")),
        P("lon", ("lat", "section"), None),
        P("section", "lat", "lon", None, None),
        P("section", "lat", "lon", None, None),
        P("section", "lat", "lon", None, None),
        P("lat", None, None, None),
    )
    return jax.shard_map(
        per_device,
        mesh=mesh,
        in_specs=placed,
        out_specs=(
            P("section", "lat", "lon", None, None),
            P("section", "lat", "lon", None, None),
            P("section", "lat", "lon", None, None),
            P("section", "lat", "lon", None, None),
        ),
        check_vma=False,
    )
```

```python
import jax
import jax.numpy as jnp
import numpy as np
from jax import lax
from jax.experimental import pallas as pl
from jax.experimental.pallas import tpu as pltpu
from jax.sharding import PartitionSpec as P

HEADS = 24
HD = 64
TOP = 2
WIN_LON = 12
FIRST_SLOTS = 16


EPSILON = 1e-06

LANES = 2 * HD
PAIRS_AT_ONCE = 4


def split_heads(x):
    lane = lax.broadcasted_iota(jnp.int32, x.shape, 1)
    zero = jnp.zeros_like(x)
    return jnp.concatenate([jnp.where(lane < HD, x, zero), jnp.where(lane < HD, zero, x)], axis=0)


def probs_kernel(query_ref, key_ref, bias_ref, probs_ref):
    scores = lax.dot_general(
        key_ref[...],
        split_heads(query_ref[...]),
        (((1,), (1,)), ((), ())),
        preferred_element_type=jnp.float32,
    ) * (HD ** (-0.5))
    bias = jnp.concatenate([bias_ref[0].astype(jnp.float32).T, bias_ref[1].astype(jnp.float32).T], axis=1)
    scores = scores + bias
    weight = jnp.exp(scores - jnp.max(scores, axis=0, keepdims=True))
    probs_ref[0] = weight / jnp.sum(weight, axis=0, keepdims=True)


def probabilities(query, key, bias):
    points, width = query.shape
    pairs = width // LANES
    return pl.pallas_call(
        probs_kernel,
        grid=(pairs,),
        in_specs=[
            pl.BlockSpec((points, LANES), lambda i: (0, i)),
            pl.BlockSpec((points, LANES), lambda i: (0, i)),
            pl.BlockSpec((2, points, points), lambda i: (i, 0, 0)),
        ],
        out_specs=pl.BlockSpec((1, points, 2 * points), lambda i: (i, 0, 0)),
        out_shape=jax.ShapeDtypeStruct((pairs, points, 2 * points), jnp.float32),
        cost_estimate=pl.CostEstimate(flops=2 * 10**8, bytes_accessed=4 * 10**6, transcendentals=10**6),
    )(query, key, bias)


def attention_kernel(
    own_ref, west_ref, take_own_ref, take_west_ref, query_ref, key_ref, value_ref, probs_ref,
    d_query_ref, d_key_ref, d_value_ref,
):
    context = jnp.dot(take_own_ref[...], own_ref[...], preferred_element_type=jnp.float32)
    context = context + jnp.dot(take_west_ref[...], west_ref[...], preferred_element_type=jnp.float32)
    context = context.astype(jnp.bfloat16)
    scale = HD ** (-0.5)
    points = own_ref.shape[0]
    for pair in range(PAIRS_AT_ONCE):
        at = slice(pair * LANES, (pair + 1) * LANES)
        grads = split_heads(context[:, at])
        key = key_ref[:, at]
        probs = probs_ref[pair]
        d_probs = lax.dot_general(
            value_ref[:, at], grads, (((1,), (1,)), ((), ())), preferred_element_type=jnp.float32
        )
        delta = jnp.sum(probs * d_probs, axis=0, keepdims=True)
        d_scores = (probs * (d_probs - delta)).astype(jnp.bfloat16)
        d_value_ref[:, at] = jnp.dot(
            probs.astype(jnp.bfloat16), grads, preferred_element_type=jnp.float32
        ).astype(jnp.bfloat16)
        d_key_ref[:, at] = (
            jnp.dot(d_scores, split_heads(query_ref[:, at]), preferred_element_type=jnp.float32)
            * scale
        ).astype(jnp.bfloat16)
        both = lax.dot_general(
            d_scores, key, (((0,), (0,)), ((), ())), preferred_element_type=jnp.float32
        )
        lane = lax.broadcasted_iota(jnp.int32, (points, LANES), 1)
        d_query_ref[:, at] = (jnp.where(lane < HD, both[:points], both[points:]) * scale).astype(
            jnp.bfloat16
        )


def attention_grads(own, west, query, key, value, probs):
    points, width = query.shape
    half = WIN_LON // 2
    cell = np.arange(points)
    row, column = cell // WIN_LON, cell % WIN_LON
    take_own = (column < half)[:, None] & (cell[:, None] + half == cell[None, :])
    place = row * half + column - half
    take_west = (column >= half)[:, None] & (place[:, None] == np.arange(points // 2)[None, :])
    take_own = jnp.asarray(take_own, jnp.bfloat16)
    take_west = jnp.asarray(take_west, jnp.bfloat16)
    block = PAIRS_AT_ONCE * LANES
    columns = pl.BlockSpec((points, block), lambda i: (0, i))
    return pl.pallas_call(
        attention_kernel,
        grid=(width // block,),
        in_specs=[
            columns,
            pl.BlockSpec((points // 2, block), lambda i: (0, i)),
            pl.BlockSpec(take_own.shape, lambda i: (0, 0)),
            pl.BlockSpec(take_west.shape, lambda i: (0, 0)),
            columns,
            columns,
            columns,
            pl.BlockSpec((PAIRS_AT_ONCE, points, 2 * points), lambda i: (i, 0, 0)),
        ],
        out_specs=[columns] * 3,
        out_shape=[jax.ShapeDtypeStruct((points, width), jnp.bfloat16)] * 3,
        cost_estimate=pl.CostEstimate(flops=5 * 10**8, bytes_accessed=6 * 10**6, transcendentals=0),
    )(own, west, take_own, take_west, query, key, value, probs)


def norm_kernel(
    own_ref, core_ref, across_ref, hidden_ref, upstream_ref, gain_ref, take_ref, grad_ref, west_ref
):
    points = own_ref.shape[0]
    grad_normed = own_ref[...] + core_ref[:points].astype(jnp.float32)
    grad_normed = grad_normed + across_ref[...].astype(jnp.float32)
    hidden = hidden_ref[...].astype(jnp.float32)
    inverse = lax.rsqrt(jnp.mean(hidden * hidden, axis=-1, keepdims=True) + EPSILON)
    normed = hidden * inverse
    d_normed = grad_normed * gain_ref[...]
    inner = jnp.mean(d_normed * normed, axis=-1, keepdims=True)
    grad = (
        upstream_ref[...].astype(jnp.float32) + inverse * (d_normed - normed * inner)
    ).astype(jnp.bfloat16)
    grad_ref[...] = grad
    west_ref[...] = jnp.dot(
        take_ref[...], grad, preferred_element_type=jnp.float32
    ).astype(jnp.bfloat16)


def norm_grads(own, core, across, hidden, upstream, gain):
    points, width = hidden.shape
    half = WIN_LON // 2
    kept = np.arange(points // 2)
    take = (kept // half * WIN_LON + kept % half)[:, None] == np.arange(points)[None, :]
    return pl.pallas_call(
        norm_kernel,
        out_shape=[
            jax.ShapeDtypeStruct((points, width), jnp.bfloat16),
            jax.ShapeDtypeStruct((points // 2, width), jnp.bfloat16),
        ],
        compiler_params=pltpu.CompilerParams(vmem_limit_bytes=32 * 2**20),
        cost_estimate=pl.CostEstimate(flops=3 * 10**8, bytes_accessed=4 * 10**6, transcendentals=0),
    )(own, core, across, hidden, upstream, gain.reshape(1, width), jnp.asarray(take, jnp.bfloat16))


def select_kernel(row_ref, code_ref, weight_ref, *refs):
    token_refs, out_refs = refs[:4], refs[4:]
    first = row_ref[...] == code_ref[0:1, :]
    second = row_ref[...] == code_ref[1:2, :]
    weight = jnp.sum(
        jnp.where(first, weight_ref[0:1, :], 0.0) + jnp.where(second, weight_ref[1:2, :], 0.0),
        axis=1,
        keepdims=True,
    )
    chosen = jnp.where(first | second, 1.0, 0.0).astype(jnp.bfloat16)
    tokens = jnp.concatenate([ref[...] for ref in token_refs], axis=0)
    rows = jnp.dot(chosen, tokens, preferred_element_type=jnp.float32)
    rows = (rows * weight).astype(jnp.bfloat16)
    size = rows.shape[0] // len(out_refs)
    for at, out_ref in enumerate(out_refs):
        out_ref[...] = rows[at * size : (at + 1) * size]


def select_rows(row_codes, codes, weights, tokens):
    size = row_codes.shape[0] // 4
    width = tokens[0].shape[1]
    return pl.pallas_call(
        select_kernel,
        out_shape=[jax.ShapeDtypeStruct((size, width), jnp.bfloat16)] * 4,
        compiler_params=pltpu.CompilerParams(vmem_limit_bytes=32 * 2**20),
        cost_estimate=pl.CostEstimate(flops=10**9, bytes_accessed=4 * 10**6, transcendentals=0),
    )(row_codes, codes, weights, *tokens)


def gather_kernel(place_ref, *refs):
    block_refs, out_refs = refs[:4], refs[4:]
    blocks = jnp.concatenate([ref[...] for ref in block_refs], axis=0)
    rows = jnp.dot(place_ref[...], blocks, preferred_element_type=jnp.float32).astype(jnp.bfloat16)
    at = 0
    for out_ref in out_refs:
        whole = out_ref.shape[0] == rows.shape[0]
        out_ref[...] = rows if whole else rows[at : at + out_ref.shape[0]]
        at += 0 if whole else out_ref.shape[0]


def placed_rows(place, blocks, sizes):
    width = blocks[0].shape[1]
    return pl.pallas_call(
        gather_kernel,
        out_shape=[jax.ShapeDtypeStruct((size, width), jnp.bfloat16) for size in sizes],
        compiler_params=pltpu.CompilerParams(vmem_limit_bytes=32 * 2**20),
        cost_estimate=pl.CostEstimate(flops=10**9, bytes_accessed=4 * 10**6, transcendentals=0),
    )(place, *blocks)


def scatter_kernel(place_ref, rows_ref, *out_refs):
    rows = jnp.dot(place_ref[...], rows_ref[...], preferred_element_type=jnp.float32)
    rows = rows.astype(jnp.bfloat16)
    size = rows.shape[0] // len(out_refs)
    for at, out_ref in enumerate(out_refs):
        out_ref[...] = rows[at * size : (at + 1) * size]


def split_rows(place, rows):
    size = place.shape[0] // 4
    return pl.pallas_call(
        scatter_kernel,
        out_shape=[jax.ShapeDtypeStruct((size, rows.shape[1]), jnp.bfloat16)] * 4,
        compiler_params=pltpu.CompilerParams(vmem_limit_bytes=32 * 2**20),
        cost_estimate=pl.CostEstimate(flops=10**9, bytes_accessed=4 * 10**6, transcendentals=0),
    )(place, rows)


def combine_kernel(chosen_ref, *refs):
    block_refs = refs[:4]
    own_ref, across_ref, core_ref = refs[4:]
    blocks = jnp.concatenate([ref[...] for ref in block_refs], axis=0)
    sums = jnp.dot(chosen_ref[...], blocks, preferred_element_type=jnp.float32)
    size = own_ref.shape[0]
    own_ref[...] = sums[:size]
    across_ref[...] = sums[2 * size : 3 * size]
    core_ref[:size] = sums[size : 2 * size].astype(jnp.bfloat16)
    core_ref[size:] = sums[3 * size :].astype(jnp.bfloat16)


def combine_rows(chosen, blocks):
    size, width = chosen.shape[0] // 4, blocks[0].shape[1]
    return pl.pallas_call(
        combine_kernel,
        out_shape=[
            jax.ShapeDtypeStruct((size, width), jnp.float32),
            jax.ShapeDtypeStruct((size, width), jnp.float32),
            jax.ShapeDtypeStruct((2 * size, width), jnp.bfloat16),
        ],
        compiler_params=pltpu.CompilerParams(vmem_limit_bytes=32 * 2**20),
        cost_estimate=pl.CostEstimate(flops=10**9, bytes_accessed=4 * 10**6, transcendentals=0),
    )(chosen, *blocks)


def passed_along(x, axis, by):
    devices = lax.axis_size(axis)
    return lax.ppermute(x, axis, [(i, (i + by) % devices) for i in range(devices)])


def expert_term(incoming, gate_rows, up_rows, gate_mat, up_mat, down_mat):
    contract = (((1,), (1,)), ((), ()))
    back_grad = lax.dot_general(incoming, down_mat, contract, preferred_element_type=jnp.float32)
    gate_pre = gate_rows.astype(jnp.float32)
    up_pre = up_rows.astype(jnp.float32)
    sigma = jax.nn.sigmoid(gate_pre)
    d_gate = (back_grad * up_pre * sigma * (1.0 + gate_pre * (1.0 - sigma))).astype(jnp.bfloat16)
    d_up = (back_grad * gate_pre * sigma).astype(jnp.bfloat16)
    total = lax.dot_general(d_gate, gate_mat, contract, preferred_element_type=jnp.float32)
    return total + lax.dot_general(d_up, up_mat, contract, preferred_element_type=jnp.float32)


def per_device(
    residual_stream,
    grad_out,
    norm_gain,
    expert_ids,
    route_weights,
    gate_saved,
    up_saved,
    gate_weight,
    up_weight,
    down_weight,
    queries,
    key_states,
    value_states,
    window_bias,
):
    lon_count = lax.axis_size("lon")
    lat_count = lax.axis_size("lat")
    section_count = lax.axis_size("section")
    windows = residual_stream.shape[2]
    points = residual_stream.shape[3]
    width = residual_stream.shape[4]
    tok_rows = windows * points
    capacity = gate_saved.shape[4]
    shard_width = gate_saved.shape[5]
    route_count = tok_rows * TOP
    upstream = grad_out.reshape(tok_rows, width)
    lon = lax.axis_index("lon")
    x_place, corner = lon // 4, lax.rem(lon, 4)

    def swapped(x, bit):
        return lax.ppermute(x, "lon", [(i, i ^ bit) for i in range(lon_count)])

    def along_x(x, by):
        return lax.ppermute(x, "lon", [(i, (i + 4 * by) % lon_count) for i in range(lon_count)])

    across = swapped(upstream, 2)
    chosen = expert_ids.reshape(tok_rows, TOP).T
    flat = chosen.T.reshape(route_count)
    onehot = (flat[:, None] == jnp.arange(lon_count, dtype=jnp.int32)[None, :]).astype(jnp.int32)
    slot_of = jnp.sum((jnp.cumsum(onehot, axis=0) - onehot) * onehot, axis=1)
    slot_of = slot_of.reshape(tok_rows, TOP).T
    code = (chosen * 32 + slot_of) * 4 + corner
    facts = jnp.concatenate(
        [code.astype(jnp.float32), route_weights.reshape(tok_rows, TOP).T], axis=0
    )
    facts_across = swapped(facts, 2)
    facts_core = swapped(facts, 1)
    core = swapped(upstream, 1)
    facts_both = swapped(facts_across, 1)
    both = swapped(across, 1)
    facts = jnp.concatenate([facts, facts_core, facts_across, facts_both], axis=1)
    slots = capacity + 1
    steps = (0, 1, -1, 2)
    row = jnp.arange(4 * slots, dtype=jnp.int32)
    row_codes = jnp.concatenate(
        [
            ((lax.rem(x_place + step + 4, 4) * 4 + corner) * 32 + row // 4) * 4 + row % 4
            for step in steps
        ]
    )
    codes = facts[:TOP].astype(jnp.int32)
    blocks = select_rows(
        row_codes.reshape(16 * slots, 1), codes, facts[TOP:], (upstream, core, across, both)
    )
    blocks = [blocks[0]] + [along_x(blocks[at], steps[at]) for at in (1, 2, 3)]
    came = jnp.concatenate(
        [row // 4 * 16 + lax.rem(x_place - step + 4, 4) * 4 + row % 4 for step in steps]
    )
    places = jnp.arange(lon_count * capacity, dtype=jnp.int32)
    place = (places[:, None] == came[None, :]).astype(jnp.bfloat16)
    first = FIRST_SLOTS * lon_count
    arrived, high, low = placed_rows(
        place, blocks, (lon_count * capacity, first, lon_count * capacity - first)
    )
    gate_mat = gate_weight[0]
    up_mat = up_weight[0]
    down_mat = down_weight[0]
    gate_flat = gate_saved[0].transpose(0, 1, 3, 2, 4).reshape(
        lat_count, section_count, lon_count * capacity, shard_width
    )
    up_flat = up_saved[0].transpose(0, 1, 3, 2, 4).reshape(
        lat_count, section_count, lon_count * capacity, shard_width
    )
    lat = lax.axis_index("lat")
    section = lax.axis_index("section")

    def term(incoming, lat_step, section_step, low, high):
        at = (lax.rem(lat - lat_step + lat_count, lat_count), section ^ section_step, low, 0)
        size = (1, 1, high - low, shard_width)
        gate_rows = lax.dynamic_slice(gate_flat, at, size)[0, 0]
        up_rows = lax.dynamic_slice(up_flat, at, size)[0, 0]
        return expert_term(incoming, gate_rows, up_rows, gate_mat, up_mat, down_mat)

    count = lon_count * capacity
    half = count // 2
    half_high = first // 2
    landed = []

    def start(x, way):
        if landed:
            x = lax.optimization_barrier((x,) + tuple(landed))[0]
        if way:
            return passed_along(x, "lat", way)
        return passed_along(x, "section", 1)

    def both_ways(up, down):
        return start(up, 1), start(down, -1)

    def land(*arrays):
        landed.extend(arrays)
        del landed[:-4]

    def rounded(x):
        return x.astype(jnp.bfloat16)

    def widened(x):
        return x.astype(jnp.float32)

    def low_term(rows, step, side):
        return term(rows, step, side, first, count)

    def high_term(rows, step, side):
        return term(rows, step, side, 0, first)

    def far_back(x, cut):
        x = rounded(x)
        return both_ways(x[cut:], x[:cut])

    def near_back(up, down, got, cut):
        from_down, from_up = got
        up = jnp.concatenate([up[:cut] + widened(from_up), up[cut:]], axis=0)
        down = jnp.concatenate([down[:cut], down[cut:] + widened(from_down)], axis=0)
        return both_ways(rounded(down), rounded(up))

    def summed_up(own, got):
        return own + widened(got[0]) + widened(got[1])

    up, down = both_ways(arrived, arrived)
    query = queries.reshape(points, width)
    key = key_states.reshape(points, width)
    probs = probabilities(query, key, window_bias[0])
    high_z = start(high, 0)
    land(high_z, probs)
    low_z = start(low, 0)
    land(up, down)
    far = both_ways(up[:half], down[half:])
    high_up_z, high_down_z = both_ways(high_z, high_z)
    land(low_z)
    low_up_z = start(up[first:], 0)
    land(low_up_z)
    low_down_z = start(down[first:], 0)
    land(*far)
    far = jnp.concatenate(far, axis=0)
    land(low_down_z)
    low_far_z = start(far[first:], 0)
    land(high_up_z, high_down_z)
    far_z = both_ways(high_up_z[:half_high], high_down_z[half_high:])
    land(*far_z)
    high_far_z = jnp.concatenate(far_z, axis=0)
    far_1 = far_back(high_term(high_far_z, 2, 1), half_high)
    land(low_far_z)
    crossed_far = start(rounded(low_term(low_far_z, 2, 1)), 0)
    land(*far_1)
    near_1 = near_back(
        high_term(high_up_z, 1, 1), high_term(high_down_z, -1, 1), far_1, half_high
    )
    land(crossed_far)
    crossed_up = start(rounded(low_term(low_up_z, 1, 1)), 0)
    far_0 = far_back(
        jnp.concatenate(
            [
                high_term(far[:first], 2, 0),
                low_term(far[first:], 2, 0) + widened(crossed_far),
            ],
            axis=0,
        ),
        half,
    )
    land(crossed_up)
    crossed_down = start(rounded(low_term(low_down_z, -1, 1)), 0)
    land(*near_1)
    land(*far_0)
    land(crossed_down)
    near_0 = near_back(
        jnp.concatenate(
            [
                high_term(up[:first], 1, 0),
                low_term(up[first:], 1, 0) + widened(crossed_up),
            ],
            axis=0,
        ),
        jnp.concatenate(
            [
                high_term(down[:first], -1, 0),
                low_term(down[first:], -1, 0) + widened(crossed_down),
            ],
            axis=0,
        ),
        far_0,
        half,
    )
    crossed_high = start(rounded(summed_up(high_term(high_z, 0, 1), near_1)), 0)
    land(crossed_high)
    crossed_low = start(rounded(low_term(low_z, 0, 1)), 0)
    crossed = jnp.concatenate([crossed_high, crossed_low], axis=0)
    own = jnp.concatenate([high_term(high, 0, 0), low_term(low, 0, 0)], axis=0)
    summed = rounded(summed_up(own + widened(crossed), near_0))
    returned = split_rows((came[:, None] == places[None, :]).astype(jnp.bfloat16), summed)
    returned = [returned[0]] + [along_x(returned[at], -steps[at]) for at in (1, 2, 3)]
    combine = (
        (codes[0][:, None] == row_codes[None, :]) | (codes[1][:, None] == row_codes[None, :])
    ).astype(jnp.bfloat16)
    own_sum, across_sum, core_sum = combine_rows(combine, returned)
    core_sum = swapped(core_sum, 1)
    across_sum = rounded(across_sum + widened(core_sum[tok_rows:]))
    across_sum = swapped(across_sum, 2)
    grad_hidden, west = norm_grads(
        own_sum,
        core_sum,
        across_sum,
        residual_stream.reshape(points, width),
        upstream,
        norm_gain,
    )
    west = passed_along(west, "lon", -1)
    grad_queries, grad_keys, grad_values = attention_grads(
        grad_hidden, west, query, key, value_states.reshape(points, width), probs
    )
    out_shape = residual_stream.shape
    return (
        grad_hidden.reshape(out_shape),
        grad_queries.reshape(out_shape),
        grad_keys.reshape(out_shape),
        grad_values.reshape(out_shape),
    )


def solution(mesh):
    placed = (
        P("section", "lat", "lon", None, None),
        P("section", "lat", "lon", None, None),
        P(),
        P("section", "lat", "lon", None, None),
        P("section", "lat", "lon", None, None),
        P("lon", None, None, None, None, ("lat", "section")),
        P("lon", None, None, None, None, ("lat", "section")),
        P("lon", None, ("lat", "section")),
        P("lon", None, ("lat", "section")),
        P("lon", ("lat", "section"), None),
        P("section", "lat", "lon", None, None),
        P("section", "lat", "lon", None, None),
        P("section", "lat", "lon", None, None),
        P("lat", None, None, None),
    )
    return jax.shard_map(
        per_device,
        mesh=mesh,
        in_specs=placed,
        out_specs=(
            P("section", "lat", "lon", None, None),
            P("section", "lat", "lon", None, None),
            P("section", "lat", "lon", None, None),
            P("section", "lat", "lon", None, None),
        ),
        check_vma=False,
    )
```

```python
import jax
import jax.numpy as jnp
import numpy as np
from jax import lax
from jax.experimental import pallas as pl
from jax.experimental.pallas import tpu as pltpu
from jax.sharding import PartitionSpec as P

HEADS = 24
HD = 64
TOP = 2
WIN_LON = 12
FIRST_SLOTS = 16


EPSILON = 1e-06

LANES = 2 * HD
PAIRS_AT_ONCE = 4


def split_heads(x):
    lane = lax.broadcasted_iota(jnp.int32, x.shape, 1)
    zero = jnp.zeros_like(x)
    return jnp.concatenate([jnp.where(lane < HD, x, zero), jnp.where(lane < HD, zero, x)], axis=0)


def probs_kernel(query_ref, key_ref, bias_ref, probs_ref):
    for pair in range(PAIRS_AT_ONCE):
        at = slice(pair * LANES, (pair + 1) * LANES)
        scores = lax.dot_general(
            key_ref[:, at],
            split_heads(query_ref[:, at]),
            (((1,), (1,)), ((), ())),
            preferred_element_type=jnp.float32,
        ) * (HD ** (-0.5))
        bias = [bias_ref[2 * pair + head].astype(jnp.float32).T for head in (0, 1)]
        scores = scores + jnp.concatenate(bias, axis=1)
        weight = jnp.exp(scores - jnp.max(scores, axis=0, keepdims=True))
        probs_ref[pair] = weight * (1.0 / jnp.sum(weight, axis=0, keepdims=True))


def probabilities(query, key, bias):
    points, width = query.shape
    pairs = width // LANES
    block = PAIRS_AT_ONCE * LANES
    return pl.pallas_call(
        probs_kernel,
        grid=(pairs // PAIRS_AT_ONCE,),
        in_specs=[
            pl.BlockSpec((points, block), lambda i: (0, i)),
            pl.BlockSpec((points, block), lambda i: (0, i)),
            pl.BlockSpec((2 * PAIRS_AT_ONCE, points, points), lambda i: (i, 0, 0)),
        ],
        out_specs=pl.BlockSpec((PAIRS_AT_ONCE, points, 2 * points), lambda i: (i, 0, 0)),
        out_shape=jax.ShapeDtypeStruct((pairs, points, 2 * points), jnp.float32),
        compiler_params=pltpu.CompilerParams(vmem_limit_bytes=32 * 2**20),
        cost_estimate=pl.CostEstimate(flops=2 * 10**8, bytes_accessed=4 * 10**6, transcendentals=10**6),
    )(query, key, bias)


def attention_kernel(
    own_ref, west_ref, take_own_ref, take_west_ref, query_ref, key_ref, value_ref, probs_ref,
    d_query_ref, d_key_ref, d_value_ref,
):
    context = jnp.dot(take_own_ref[...], own_ref[...], preferred_element_type=jnp.float32)
    context = context + jnp.dot(take_west_ref[...], west_ref[...], preferred_element_type=jnp.float32)
    context = context.astype(jnp.bfloat16)
    scale = HD ** (-0.5)
    points = own_ref.shape[0]
    for pair in range(PAIRS_AT_ONCE):
        at = slice(pair * LANES, (pair + 1) * LANES)
        grads = split_heads(context[:, at])
        key = key_ref[:, at]
        probs = probs_ref[pair]
        d_probs = lax.dot_general(
            value_ref[:, at], grads, (((1,), (1,)), ((), ())), preferred_element_type=jnp.float32
        )
        delta = jnp.sum(probs * d_probs, axis=0, keepdims=True)
        d_scores = (probs * (d_probs - delta)).astype(jnp.bfloat16)
        d_value_ref[:, at] = jnp.dot(
            probs.astype(jnp.bfloat16), grads, preferred_element_type=jnp.float32
        ).astype(jnp.bfloat16)
        d_key_ref[:, at] = (
            jnp.dot(d_scores, split_heads(query_ref[:, at]), preferred_element_type=jnp.float32)
            * scale
        ).astype(jnp.bfloat16)
        both = lax.dot_general(
            d_scores, key, (((0,), (0,)), ((), ())), preferred_element_type=jnp.float32
        )
        lane = lax.broadcasted_iota(jnp.int32, (points, LANES), 1)
        d_query_ref[:, at] = (jnp.where(lane < HD, both[:points], both[points:]) * scale).astype(
            jnp.bfloat16
        )


def attention_grads(own, west, query, key, value, probs):
    points, width = query.shape
    half = WIN_LON // 2
    cell = np.arange(points)
    row, column = cell // WIN_LON, cell % WIN_LON
    take_own = (column < half)[:, None] & (cell[:, None] + half == cell[None, :])
    place = row * half + column - half
    take_west = (column >= half)[:, None] & (place[:, None] == np.arange(points // 2)[None, :])
    take_own = jnp.asarray(take_own, jnp.bfloat16)
    take_west = jnp.asarray(take_west, jnp.bfloat16)
    block = PAIRS_AT_ONCE * LANES
    columns = pl.BlockSpec((points, block), lambda i: (0, i))
    return pl.pallas_call(
        attention_kernel,
        grid=(width // block,),
        in_specs=[
            columns,
            pl.BlockSpec((points // 2, block), lambda i: (0, i)),
            pl.BlockSpec(take_own.shape, lambda i: (0, 0)),
            pl.BlockSpec(take_west.shape, lambda i: (0, 0)),
            columns,
            columns,
            columns,
            pl.BlockSpec((PAIRS_AT_ONCE, points, 2 * points), lambda i: (i, 0, 0)),
        ],
        out_specs=[columns] * 3,
        out_shape=[jax.ShapeDtypeStruct((points, width), jnp.bfloat16)] * 3,
        cost_estimate=pl.CostEstimate(flops=5 * 10**8, bytes_accessed=6 * 10**6, transcendentals=0),
    )(own, west, take_own, take_west, query, key, value, probs)


def norm_kernel(
    own_ref, core_ref, across_ref, hidden_ref, upstream_ref, gain_ref, take_ref, grad_ref, west_ref
):
    points = own_ref.shape[0]
    grad_normed = own_ref[...] + core_ref[:points].astype(jnp.float32)
    grad_normed = grad_normed + across_ref[...].astype(jnp.float32)
    hidden = hidden_ref[...].astype(jnp.float32)
    inverse = lax.rsqrt(jnp.mean(hidden * hidden, axis=-1, keepdims=True) + EPSILON)
    normed = hidden * inverse
    d_normed = grad_normed * gain_ref[...]
    inner = jnp.mean(d_normed * normed, axis=-1, keepdims=True)
    grad = (
        upstream_ref[...].astype(jnp.float32) + inverse * (d_normed - normed * inner)
    ).astype(jnp.bfloat16)
    grad_ref[...] = grad
    west_ref[...] = jnp.dot(
        take_ref[...], grad, preferred_element_type=jnp.float32
    ).astype(jnp.bfloat16)


def norm_grads(own, core, across, hidden, upstream, gain):
    points, width = hidden.shape
    half = WIN_LON // 2
    kept = np.arange(points // 2)
    take = (kept // half * WIN_LON + kept % half)[:, None] == np.arange(points)[None, :]
    return pl.pallas_call(
        norm_kernel,
        out_shape=[
            jax.ShapeDtypeStruct((points, width), jnp.bfloat16),
            jax.ShapeDtypeStruct((points // 2, width), jnp.bfloat16),
        ],
        compiler_params=pltpu.CompilerParams(vmem_limit_bytes=32 * 2**20),
        cost_estimate=pl.CostEstimate(flops=3 * 10**8, bytes_accessed=4 * 10**6, transcendentals=0),
    )(own, core, across, hidden, upstream, gain.reshape(1, width), jnp.asarray(take, jnp.bfloat16))


def select_kernel(row_ref, *refs):
    fact_refs, token_refs, code_ref, out_refs = refs[:4], refs[4:8], refs[8], refs[9:]
    points = token_refs[0].shape[0]
    before = lax.broadcasted_iota(jnp.int32, (points, points), 0) < lax.broadcasted_iota(
        jnp.int32, (points, points), 1
    )
    before = jnp.where(before, 1.0, 0.0).astype(jnp.bfloat16)
    row = row_ref[...]
    weight = jnp.zeros(row.shape, jnp.float32)
    rows = jnp.zeros((row.shape[0], token_refs[0].shape[1]), jnp.float32)
    for source in range(4):
        facts = fact_refs[source][...]
        expert = lax.broadcasted_iota(jnp.int32, (16, points), 0).astype(jnp.float32)
        marks = [jnp.where(facts[k : k + 1] == expert, 1.0, 0.0) for k in range(TOP)]
        seen = jnp.dot(
            (marks[0] + marks[1]).astype(jnp.bfloat16), before, preferred_element_type=jnp.float32
        )
        chosen = jnp.zeros((row.shape[0], points), jnp.float32)
        for k in range(TOP):
            slot = jnp.sum(marks[k] * seen, axis=0, keepdims=True)
            code = (facts[k : k + 1] * 32.0 + slot) * 4.0 + facts[4:5]
            code_ref[TOP * source + k : TOP * source + k + 1] = code
            match = jnp.where(row == code, 1.0, 0.0)
            weight = weight + jnp.sum(match * facts[TOP + k : TOP + k + 1], axis=1, keepdims=True)
            chosen = chosen + match
        rows = rows + jnp.dot(
            chosen.astype(jnp.bfloat16), token_refs[source][...], preferred_element_type=jnp.float32
        )
    rows = (rows * weight).astype(jnp.bfloat16)
    at = 0
    for out_ref in out_refs:
        out_ref[...] = rows[at : at + out_ref.shape[0]]
        at += out_ref.shape[0]


def select_rows(row_codes, facts, tokens, sizes):
    points, width = tokens[0].shape
    return pl.pallas_call(
        select_kernel,
        out_shape=[jax.ShapeDtypeStruct((4 * TOP, points), jnp.float32)]
        + [jax.ShapeDtypeStruct((size, width), jnp.bfloat16) for size in sizes],
        compiler_params=pltpu.CompilerParams(vmem_limit_bytes=32 * 2**20),
        cost_estimate=pl.CostEstimate(flops=10**9, bytes_accessed=4 * 10**6, transcendentals=0),
    )(row_codes, *facts, *tokens)


def gather_kernel(place_ref, *refs):
    block_refs, out_refs = refs[:4], refs[4:]
    blocks = jnp.concatenate([ref[...] for ref in block_refs], axis=0)
    rows = jnp.dot(place_ref[...], blocks, preferred_element_type=jnp.float32).astype(jnp.bfloat16)
    at = 0
    for out_ref in out_refs:
        whole = out_ref.shape[0] == rows.shape[0]
        out_ref[...] = rows if whole else rows[at : at + out_ref.shape[0]]
        at += 0 if whole else out_ref.shape[0]


def placed_rows(place, blocks, sizes):
    width = blocks[0].shape[1]
    return pl.pallas_call(
        gather_kernel,
        out_shape=[jax.ShapeDtypeStruct((size, width), jnp.bfloat16) for size in sizes],
        compiler_params=pltpu.CompilerParams(vmem_limit_bytes=32 * 2**20),
        cost_estimate=pl.CostEstimate(flops=10**9, bytes_accessed=4 * 10**6, transcendentals=0),
    )(place, *blocks)


def scatter_kernel(place_ref, rows_ref, *out_refs):
    rows = jnp.dot(place_ref[...], rows_ref[...], preferred_element_type=jnp.float32)
    rows = rows.astype(jnp.bfloat16)
    size = rows.shape[0] // len(out_refs)
    for at, out_ref in enumerate(out_refs):
        out_ref[...] = rows[at * size : (at + 1) * size]


def split_rows(place, rows):
    size = place.shape[0] // 4
    return pl.pallas_call(
        scatter_kernel,
        out_shape=[jax.ShapeDtypeStruct((size, rows.shape[1]), jnp.bfloat16)] * 4,
        compiler_params=pltpu.CompilerParams(vmem_limit_bytes=32 * 2**20),
        cost_estimate=pl.CostEstimate(flops=10**9, bytes_accessed=4 * 10**6, transcendentals=0),
    )(place, rows)


def combine_kernel(chosen_ref, *refs):
    block_refs = refs[:4]
    own_ref, across_ref, core_ref = refs[4:]
    blocks = jnp.concatenate([ref[...] for ref in block_refs], axis=0)
    sums = jnp.dot(chosen_ref[...], blocks, preferred_element_type=jnp.float32)
    size = own_ref.shape[0]
    own_ref[...] = sums[:size]
    across_ref[...] = sums[2 * size : 3 * size]
    core_ref[:size] = sums[size : 2 * size].astype(jnp.bfloat16)
    core_ref[size:] = sums[3 * size :].astype(jnp.bfloat16)


def combine_rows(chosen, blocks):
    size, width = chosen.shape[0] // 4, blocks[0].shape[1]
    return pl.pallas_call(
        combine_kernel,
        out_shape=[
            jax.ShapeDtypeStruct((size, width), jnp.float32),
            jax.ShapeDtypeStruct((size, width), jnp.float32),
            jax.ShapeDtypeStruct((2 * size, width), jnp.bfloat16),
        ],
        compiler_params=pltpu.CompilerParams(vmem_limit_bytes=32 * 2**20),
        cost_estimate=pl.CostEstimate(flops=10**9, bytes_accessed=4 * 10**6, transcendentals=0),
    )(chosen, *blocks)


def passed_along(x, axis, by):
    devices = lax.axis_size(axis)
    return lax.ppermute(x, axis, [(i, (i + by) % devices) for i in range(devices)])


def expert_term(incoming, gate_rows, up_rows, gate_mat, up_mat, down_mat):
    contract = (((1,), (1,)), ((), ()))
    back_grad = lax.dot_general(incoming, down_mat, contract, preferred_element_type=jnp.float32)
    gate_pre = gate_rows.astype(jnp.float32)
    up_pre = up_rows.astype(jnp.float32)
    sigma = jax.nn.sigmoid(gate_pre)
    d_gate = (back_grad * up_pre * sigma * (1.0 + gate_pre * (1.0 - sigma))).astype(jnp.bfloat16)
    d_up = (back_grad * gate_pre * sigma).astype(jnp.bfloat16)
    total = lax.dot_general(d_gate, gate_mat, contract, preferred_element_type=jnp.float32)
    return total + lax.dot_general(d_up, up_mat, contract, preferred_element_type=jnp.float32)


def per_device(
    residual_stream,
    grad_out,
    norm_gain,
    expert_ids,
    route_weights,
    gate_saved,
    up_saved,
    gate_weight,
    up_weight,
    down_weight,
    queries,
    key_states,
    value_states,
    window_bias,
):
    lon_count = lax.axis_size("lon")
    lat_count = lax.axis_size("lat")
    section_count = lax.axis_size("section")
    windows = residual_stream.shape[2]
    points = residual_stream.shape[3]
    width = residual_stream.shape[4]
    tok_rows = windows * points
    capacity = gate_saved.shape[4]
    shard_width = gate_saved.shape[5]
    upstream = grad_out.reshape(tok_rows, width)
    lon = lax.axis_index("lon")
    x_place, corner = lon // 4, lax.rem(lon, 4)

    def swapped(x, bit):
        return lax.ppermute(x, "lon", [(i, i ^ bit) for i in range(lon_count)])

    def along_x(x, by):
        return lax.ppermute(x, "lon", [(i, (i + 4 * by) % lon_count) for i in range(lon_count)])

    across = swapped(upstream, 2)
    facts = jnp.concatenate(
        [
            expert_ids.reshape(tok_rows, TOP).T.astype(jnp.float32),
            route_weights.reshape(tok_rows, TOP).T,
            jnp.full((1, tok_rows), corner.astype(jnp.float32)),
        ],
        axis=0,
    )
    facts_across = swapped(facts, 2)
    core = swapped(upstream, 1)
    facts_core = swapped(facts, 1)
    facts_both = swapped(facts_across, 1)
    both = swapped(across, 1)
    slots = capacity + 1
    steps = (0, 1, -1, 2)
    row = jnp.arange(4 * slots, dtype=jnp.int32)
    row_codes = jnp.concatenate(
        [
            ((lax.rem(x_place + step + 4, 4) * 4 + corner) * 32 + row // 4) * 4 + row % 4
            for step in steps
        ]
    ).astype(jnp.float32)
    codes, *blocks = select_rows(
        row_codes.reshape(16 * slots, 1),
        (facts, facts_core, facts_across, facts_both),
        (upstream, core, across, both),
        (4 * slots,) * 4,
    )
    blocks = [blocks[0]] + [along_x(blocks[at], steps[at]) for at in (1, 2, 3)]
    combine = (
        (codes.reshape(4, TOP, tok_rows, 1) == row_codes)
        .any(axis=1)
        .reshape(4 * tok_rows, 16 * slots)
        .astype(jnp.bfloat16)
    )
    came = jnp.concatenate(
        [row // 4 * 16 + lax.rem(x_place - step + 4, 4) * 4 + row % 4 for step in steps]
    )
    places = jnp.arange(lon_count * capacity, dtype=jnp.int32)
    place = (places[:, None] == came[None, :]).astype(jnp.bfloat16)
    first = FIRST_SLOTS * lon_count
    arrived, high, low = placed_rows(
        place, blocks, (lon_count * capacity, first, lon_count * capacity - first)
    )
    gate_mat = gate_weight[0]
    up_mat = up_weight[0]
    down_mat = down_weight[0]
    gate_flat = gate_saved[0].transpose(0, 1, 3, 2, 4).reshape(
        lat_count, section_count, lon_count * capacity, shard_width
    )
    up_flat = up_saved[0].transpose(0, 1, 3, 2, 4).reshape(
        lat_count, section_count, lon_count * capacity, shard_width
    )
    lat = lax.axis_index("lat")
    section = lax.axis_index("section")

    def term(incoming, lat_step, section_step, low, high):
        at = (lax.rem(lat - lat_step + lat_count, lat_count), section ^ section_step, low, 0)
        size = (1, 1, high - low, shard_width)
        gate_rows = lax.dynamic_slice(gate_flat, at, size)[0, 0]
        up_rows = lax.dynamic_slice(up_flat, at, size)[0, 0]
        return expert_term(incoming, gate_rows, up_rows, gate_mat, up_mat, down_mat)

    count = lon_count * capacity
    half = count // 2
    half_high = first // 2
    landed = []

    def start(x, way):
        if landed:
            x = lax.optimization_barrier((x,) + tuple(landed))[0]
        if way:
            return passed_along(x, "lat", way)
        return passed_along(x, "section", 1)

    def both_ways(up, down):
        return start(up, 1), start(down, -1)

    def land(*arrays):
        landed.extend(arrays)
        del landed[:-8]

    def rounded(x):
        return x.astype(jnp.bfloat16)

    def widened(x):
        return x.astype(jnp.float32)

    def low_term(rows, step, side):
        return term(rows, step, side, first, count)

    def high_term(rows, step, side):
        return term(rows, step, side, 0, first)

    def far_back(x, cut):
        x = rounded(x)
        return both_ways(x[cut:], x[:cut])

    def near_back(up, down, got, cut):
        from_down, from_up = got
        up = jnp.concatenate([up[:cut] + widened(from_up), up[cut:]], axis=0)
        down = jnp.concatenate([down[:cut], down[cut:] + widened(from_down)], axis=0)
        return both_ways(rounded(down), rounded(up))

    def summed_up(own, got):
        return own + widened(got[0]) + widened(got[1])

    def held(x, *arrays):
        return lax.optimization_barrier((x,) + arrays)[0]

    up, down = both_ways(arrived, arrived)
    high_z = start(high, 0)
    own = jnp.concatenate([high_term(high, 0, 0), low_term(low, 0, 0)], axis=0)
    land(high_z, own)
    low_z = start(low, 0)
    query = queries.reshape(points, width)
    key = key_states.reshape(points, width)
    probs = probabilities(held(query, high_z), key, window_bias[0])
    t_high_z = high_term(high_z, 0, 1)
    land(up, down, probs, t_high_z)
    far = both_ways(up[:half], down[half:])
    land(low_z)
    low_up_z = start(up[first:], 0)
    t_up = (high_term(up[:first], 1, 0), low_term(up[first:], 1, 0))
    land(low_up_z, *t_up)
    low_down_z = start(down[first:], 0)
    high_up_z, high_down_z = both_ways(high_z, high_z)
    later = held(down, low_up_z)
    t_down = (high_term(later[:first], -1, 0), low_term(later[first:], -1, 0))
    t_low_z = low_term(held(low_z, low_up_z), 0, 1)
    land(*far, *t_down, t_low_z, low_down_z)
    far = jnp.concatenate(far, axis=0)
    low_far_z = start(far[first:], 0)
    later = held(far, low_down_z)
    t_far = (high_term(later[:first], 2, 0), low_term(later[first:], 2, 0))
    t_low_up_z = low_term(held(low_up_z, low_down_z), 1, 1)
    land(high_up_z, high_down_z, *t_far, t_low_up_z)
    far_z = both_ways(high_up_z[:half_high], high_down_z[half_high:])
    high_far_z = jnp.concatenate(far_z, axis=0)
    land(low_far_z)
    crossed_far = rounded(low_term(low_far_z, 2, 1))
    high_far_z = held(high_far_z, crossed_far)
    crossed_far = start(crossed_far, 0)
    far_1 = rounded(high_term(high_far_z, 2, 1))
    land(*far_z)
    far_1 = both_ways(far_1[half_high:], far_1[:half_high])
    t_up_z = high_term(held(high_up_z, crossed_far), 1, 1)
    t_down_z = high_term(held(high_down_z, crossed_far), -1, 1)
    t_low_down_z = low_term(held(low_down_z, crossed_far), -1, 1)
    land(*far_1)
    land(crossed_far)
    near_1 = near_back(t_up_z, t_down_z, far_1, half_high)
    land(crossed_far)
    crossed_up = start(rounded(t_low_up_z), 0)
    far_0 = far_back(
        jnp.concatenate(
            [
                t_far[0],
                t_far[1] + widened(crossed_far),
            ],
            axis=0,
        ),
        half,
    )
    land(crossed_up)
    crossed_down = start(rounded(t_low_down_z), 0)
    land(*near_1)
    land(*far_0)
    land(crossed_down)
    near_0 = near_back(
        jnp.concatenate(
            [
                t_up[0],
                t_up[1] + widened(crossed_up),
            ],
            axis=0,
        ),
        jnp.concatenate(
            [
                t_down[0],
                t_down[1] + widened(crossed_down),
            ],
            axis=0,
        ),
        far_0,
        half,
    )
    crossed_high = start(rounded(summed_up(t_high_z, near_1)), 0)
    land(crossed_high)
    crossed_low = start(rounded(t_low_z), 0)
    crossed = jnp.concatenate([crossed_high, crossed_low], axis=0)
    summed = rounded(summed_up(own + widened(crossed), near_0))
    returned = split_rows((came[:, None] == places[None, :]).astype(jnp.bfloat16), summed)
    returned = [returned[0]] + [along_x(returned[at], -steps[at]) for at in (1, 2, 3)]
    own_sum, across_sum, core_sum = combine_rows(combine, returned)
    core_sum = swapped(core_sum, 1)
    across_sum = rounded(across_sum + widened(core_sum[tok_rows:]))
    across_sum = swapped(across_sum, 2)
    grad_hidden, west = norm_grads(
        own_sum,
        core_sum,
        across_sum,
        residual_stream.reshape(points, width),
        upstream,
        norm_gain,
    )
    west = passed_along(west, "lon", -1)
    grad_queries, grad_keys, grad_values = attention_grads(
        grad_hidden, west, query, key, value_states.reshape(points, width), probs
    )
    out_shape = residual_stream.shape
    return (
        grad_hidden.reshape(out_shape),
        grad_queries.reshape(out_shape),
        grad_keys.reshape(out_shape),
        grad_values.reshape(out_shape),
    )


def solution(mesh):
    placed = (
        P("section", "lat", "lon", None, None),
        P("section", "lat", "lon", None, None),
        P(),
        P("section", "lat", "lon", None, None),
        P("section", "lat", "lon", None, None),
        P("lon", None, None, None, None, ("lat", "section")),
        P("lon", None, None, None, None, ("lat", "section")),
        P("lon", None, ("lat", "section")),
        P("lon", None, ("lat", "section")),
        P("lon", ("lat", "section"), None),
        P("section", "lat", "lon", None, None),
        P("section", "lat", "lon", None, None),
        P("section", "lat", "lon", None, None),
        P("lat", None, None, None),
    )
    return jax.shard_map(
        per_device,
        mesh=mesh,
        in_specs=placed,
        out_specs=(
            P("section", "lat", "lon", None, None),
            P("section", "lat", "lon", None, None),
            P("section", "lat", "lon", None, None),
            P("section", "lat", "lon", None, None),
        ),
        check_vma=False,
    )
```

```python
import jax
import jax.numpy as jnp
import numpy as np
from jax import lax
from jax.experimental import pallas as pl
from jax.experimental.pallas import tpu as pltpu
from jax.sharding import PartitionSpec as P

HEADS = 24
HD = 64
TOP = 2
WIN_LON = 12
FIRST_SLOTS = 16


EPSILON = 1e-06

LANES = 2 * HD
PAIRS_AT_ONCE = 4
ATTENTION_PAIRS = 12


def split_heads(x):
    lane = lax.broadcasted_iota(jnp.int32, x.shape, 1)
    zero = jnp.zeros_like(x)
    return jnp.concatenate([jnp.where(lane < HD, x, zero), jnp.where(lane < HD, zero, x)], axis=0)


def probs_kernel(query_ref, key_ref, bias_ref, probs_ref):
    for pair in range(PAIRS_AT_ONCE):
        at = slice(pair * LANES, (pair + 1) * LANES)
        scores = lax.dot_general(
            key_ref[:, at],
            split_heads(query_ref[:, at]),
            (((1,), (1,)), ((), ())),
            preferred_element_type=jnp.float32,
        ) * (HD ** (-0.5))
        bias = [bias_ref[2 * pair + head].astype(jnp.float32).T for head in (0, 1)]
        scores = scores + jnp.concatenate(bias, axis=1)
        weight = jnp.exp(scores - jnp.max(scores, axis=0, keepdims=True))
        probs_ref[pair] = weight * (1.0 / jnp.sum(weight, axis=0, keepdims=True))


def probabilities(query, key, bias):
    points, width = query.shape
    pairs = width // LANES
    block = PAIRS_AT_ONCE * LANES
    return pl.pallas_call(
        probs_kernel,
        grid=(pairs // PAIRS_AT_ONCE,),
        in_specs=[
            pl.BlockSpec((points, block), lambda i: (0, i)),
            pl.BlockSpec((points, block), lambda i: (0, i)),
            pl.BlockSpec((2 * PAIRS_AT_ONCE, points, points), lambda i: (i, 0, 0)),
        ],
        out_specs=pl.BlockSpec((PAIRS_AT_ONCE, points, 2 * points), lambda i: (i, 0, 0)),
        out_shape=jax.ShapeDtypeStruct((pairs, points, 2 * points), jnp.float32),
        compiler_params=pltpu.CompilerParams(vmem_limit_bytes=32 * 2**20),
        cost_estimate=pl.CostEstimate(flops=2 * 10**8, bytes_accessed=4 * 10**6, transcendentals=10**6),
    )(query, key, bias)


def attention_kernel(
    own_ref, west_ref, take_own_ref, take_west_ref, query_ref, key_ref, value_ref, probs_ref,
    d_query_ref, d_key_ref, d_value_ref,
):
    context = jnp.dot(take_own_ref[...], own_ref[...], preferred_element_type=jnp.float32)
    context = context + jnp.dot(take_west_ref[...], west_ref[...], preferred_element_type=jnp.float32)
    context = context.astype(jnp.bfloat16)
    scale = HD ** (-0.5)
    points = own_ref.shape[0]
    for pair in range(ATTENTION_PAIRS):
        at = slice(pair * LANES, (pair + 1) * LANES)
        grads = split_heads(context[:, at])
        key = key_ref[:, at]
        probs = probs_ref[pair]
        d_probs = lax.dot_general(
            value_ref[:, at], grads, (((1,), (1,)), ((), ())), preferred_element_type=jnp.float32
        )
        delta = jnp.sum(probs * d_probs, axis=0, keepdims=True)
        d_scores = (probs * (d_probs - delta)).astype(jnp.bfloat16)
        d_value_ref[:, at] = jnp.dot(
            probs.astype(jnp.bfloat16), grads, preferred_element_type=jnp.float32
        ).astype(jnp.bfloat16)
        d_key_ref[:, at] = (
            jnp.dot(d_scores, split_heads(query_ref[:, at]), preferred_element_type=jnp.float32)
            * scale
        ).astype(jnp.bfloat16)
        both = lax.dot_general(
            d_scores, key, (((0,), (0,)), ((), ())), preferred_element_type=jnp.float32
        )
        lane = lax.broadcasted_iota(jnp.int32, (points, LANES), 1)
        d_query_ref[:, at] = (jnp.where(lane < HD, both[:points], both[points:]) * scale).astype(
            jnp.bfloat16
        )


def attention_grads(own, west, query, key, value, probs):
    points, width = query.shape
    half = WIN_LON // 2
    cell = np.arange(points)
    row, column = cell // WIN_LON, cell % WIN_LON
    take_own = (column < half)[:, None] & (cell[:, None] + half == cell[None, :])
    place = row * half + column - half
    take_west = (column >= half)[:, None] & (place[:, None] == np.arange(points // 2)[None, :])
    take_own = jnp.asarray(take_own, jnp.bfloat16)
    take_west = jnp.asarray(take_west, jnp.bfloat16)
    block = ATTENTION_PAIRS * LANES
    columns = pl.BlockSpec((points, block), lambda i: (0, i))
    return pl.pallas_call(
        attention_kernel,
        grid=(width // block,),
        in_specs=[
            columns,
            pl.BlockSpec((points // 2, block), lambda i: (0, i)),
            pl.BlockSpec(take_own.shape, lambda i: (0, 0)),
            pl.BlockSpec(take_west.shape, lambda i: (0, 0)),
            columns,
            columns,
            columns,
            pl.BlockSpec((ATTENTION_PAIRS, points, 2 * points), lambda i: (i, 0, 0)),
        ],
        out_specs=[columns] * 3,
        out_shape=[jax.ShapeDtypeStruct((points, width), jnp.bfloat16)] * 3,
        compiler_params=pltpu.CompilerParams(vmem_limit_bytes=32 * 2**20),
        cost_estimate=pl.CostEstimate(flops=5 * 10**8, bytes_accessed=6 * 10**6, transcendentals=0),
    )(own, west, take_own, take_west, query, key, value, probs)


def norm_kernel(
    own_ref, core_ref, across_ref, hidden_ref, upstream_ref, gain_ref, take_ref, grad_ref, west_ref
):
    points = own_ref.shape[0]
    grad_normed = own_ref[...] + core_ref[:points].astype(jnp.float32)
    grad_normed = grad_normed + across_ref[...].astype(jnp.float32)
    hidden = hidden_ref[...].astype(jnp.float32)
    inverse = lax.rsqrt(jnp.mean(hidden * hidden, axis=-1, keepdims=True) + EPSILON)
    normed = hidden * inverse
    d_normed = grad_normed * gain_ref[...]
    inner = jnp.mean(d_normed * normed, axis=-1, keepdims=True)
    grad = (
        upstream_ref[...].astype(jnp.float32) + inverse * (d_normed - normed * inner)
    ).astype(jnp.bfloat16)
    grad_ref[...] = grad
    west_ref[...] = jnp.dot(
        take_ref[...], grad, preferred_element_type=jnp.float32
    ).astype(jnp.bfloat16)


def norm_grads(own, core, across, hidden, upstream, gain):
    points, width = hidden.shape
    half = WIN_LON // 2
    kept = np.arange(points // 2)
    take = (kept // half * WIN_LON + kept % half)[:, None] == np.arange(points)[None, :]
    return pl.pallas_call(
        norm_kernel,
        out_shape=[
            jax.ShapeDtypeStruct((points, width), jnp.bfloat16),
            jax.ShapeDtypeStruct((points // 2, width), jnp.bfloat16),
        ],
        compiler_params=pltpu.CompilerParams(vmem_limit_bytes=32 * 2**20),
        cost_estimate=pl.CostEstimate(flops=3 * 10**8, bytes_accessed=4 * 10**6, transcendentals=0),
    )(own, core, across, hidden, upstream, gain.reshape(1, width), jnp.asarray(take, jnp.bfloat16))


def select_kernel(row_ref, *refs):
    fact_refs, token_refs, code_ref, out_refs = refs[:4], refs[4:8], refs[8], refs[9:]
    points = token_refs[0].shape[0]
    before = lax.broadcasted_iota(jnp.int32, (points, points), 0) < lax.broadcasted_iota(
        jnp.int32, (points, points), 1
    )
    before = jnp.where(before, 1.0, 0.0).astype(jnp.bfloat16)
    row = row_ref[...]
    weight = jnp.zeros(row.shape, jnp.float32)
    rows = jnp.zeros((row.shape[0], token_refs[0].shape[1]), jnp.float32)
    for source in range(4):
        facts = fact_refs[source][...]
        expert = lax.broadcasted_iota(jnp.int32, (16, points), 0).astype(jnp.float32)
        marks = [jnp.where(facts[k : k + 1] == expert, 1.0, 0.0) for k in range(TOP)]
        seen = jnp.dot(
            (marks[0] + marks[1]).astype(jnp.bfloat16), before, preferred_element_type=jnp.float32
        )
        chosen = jnp.zeros((row.shape[0], points), jnp.float32)
        for k in range(TOP):
            slot = jnp.sum(marks[k] * seen, axis=0, keepdims=True)
            code = (facts[k : k + 1] * 32.0 + slot) * 4.0 + facts[4:5]
            code_ref[TOP * source + k : TOP * source + k + 1] = code
            match = jnp.where(row == code, 1.0, 0.0)
            weight = weight + jnp.sum(match * facts[TOP + k : TOP + k + 1], axis=1, keepdims=True)
            chosen = chosen + match
        rows = rows + jnp.dot(
            chosen.astype(jnp.bfloat16), token_refs[source][...], preferred_element_type=jnp.float32
        )
    rows = (rows * weight).astype(jnp.bfloat16)
    at = 0
    for out_ref in out_refs:
        out_ref[...] = rows[at : at + out_ref.shape[0]]
        at += out_ref.shape[0]


def select_rows(row_codes, facts, tokens, sizes):
    points, width = tokens[0].shape
    return pl.pallas_call(
        select_kernel,
        out_shape=[jax.ShapeDtypeStruct((4 * TOP, points), jnp.float32)]
        + [jax.ShapeDtypeStruct((size, width), jnp.bfloat16) for size in sizes],
        compiler_params=pltpu.CompilerParams(vmem_limit_bytes=32 * 2**20),
        cost_estimate=pl.CostEstimate(flops=10**9, bytes_accessed=4 * 10**6, transcendentals=0),
    )(row_codes, *facts, *tokens)


def gather_kernel(place_ref, *refs):
    block_refs, out_refs = refs[:4], refs[4:]
    blocks = jnp.concatenate([ref[...] for ref in block_refs], axis=0)
    rows = jnp.dot(place_ref[...], blocks, preferred_element_type=jnp.float32).astype(jnp.bfloat16)
    at = 0
    for out_ref in out_refs:
        whole = out_ref.shape[0] == rows.shape[0]
        out_ref[...] = rows if whole else rows[at : at + out_ref.shape[0]]
        at += 0 if whole else out_ref.shape[0]


def placed_rows(place, blocks, sizes):
    width = blocks[0].shape[1]
    return pl.pallas_call(
        gather_kernel,
        out_shape=[jax.ShapeDtypeStruct((size, width), jnp.bfloat16) for size in sizes],
        compiler_params=pltpu.CompilerParams(vmem_limit_bytes=32 * 2**20),
        cost_estimate=pl.CostEstimate(flops=10**9, bytes_accessed=4 * 10**6, transcendentals=0),
    )(place, *blocks)


def scatter_kernel(place_ref, rows_ref, *out_refs):
    rows = jnp.dot(place_ref[...], rows_ref[...], preferred_element_type=jnp.float32)
    rows = rows.astype(jnp.bfloat16)
    size = rows.shape[0] // len(out_refs)
    for at, out_ref in enumerate(out_refs):
        out_ref[...] = rows[at * size : (at + 1) * size]


def split_rows(place, rows):
    size = place.shape[0] // 4
    return pl.pallas_call(
        scatter_kernel,
        out_shape=[jax.ShapeDtypeStruct((size, rows.shape[1]), jnp.bfloat16)] * 4,
        compiler_params=pltpu.CompilerParams(vmem_limit_bytes=32 * 2**20),
        cost_estimate=pl.CostEstimate(flops=10**9, bytes_accessed=4 * 10**6, transcendentals=0),
    )(place, rows)


def combine_kernel(chosen_ref, *refs):
    block_refs = refs[:4]
    own_ref, across_ref, core_ref = refs[4:]
    blocks = jnp.concatenate([ref[...] for ref in block_refs], axis=0)
    sums = jnp.dot(chosen_ref[...], blocks, preferred_element_type=jnp.float32)
    size = own_ref.shape[0]
    own_ref[...] = sums[:size]
    across_ref[...] = sums[2 * size : 3 * size]
    core_ref[:size] = sums[size : 2 * size].astype(jnp.bfloat16)
    core_ref[size:] = sums[3 * size :].astype(jnp.bfloat16)


def combine_rows(chosen, blocks):
    size, width = chosen.shape[0] // 4, blocks[0].shape[1]
    return pl.pallas_call(
        combine_kernel,
        out_shape=[
            jax.ShapeDtypeStruct((size, width), jnp.float32),
            jax.ShapeDtypeStruct((size, width), jnp.float32),
            jax.ShapeDtypeStruct((2 * size, width), jnp.bfloat16),
        ],
        compiler_params=pltpu.CompilerParams(vmem_limit_bytes=32 * 2**20),
        cost_estimate=pl.CostEstimate(flops=10**9, bytes_accessed=4 * 10**6, transcendentals=0),
    )(chosen, *blocks)


def passed_along(x, axis, by):
    devices = lax.axis_size(axis)
    return lax.ppermute(x, axis, [(i, (i + by) % devices) for i in range(devices)])


def expert_term(incoming, gate_rows, up_rows, gate_mat, up_mat, down_mat):
    contract = (((1,), (1,)), ((), ()))
    back_grad = lax.dot_general(incoming, down_mat, contract, preferred_element_type=jnp.float32)
    gate_pre = gate_rows.astype(jnp.float32)
    up_pre = up_rows.astype(jnp.float32)
    sigma = jax.nn.sigmoid(gate_pre)
    d_gate = (back_grad * up_pre * sigma * (1.0 + gate_pre * (1.0 - sigma))).astype(jnp.bfloat16)
    d_up = (back_grad * gate_pre * sigma).astype(jnp.bfloat16)
    total = lax.dot_general(d_gate, gate_mat, contract, preferred_element_type=jnp.float32)
    return total + lax.dot_general(d_up, up_mat, contract, preferred_element_type=jnp.float32)


def per_device(
    residual_stream,
    grad_out,
    norm_gain,
    expert_ids,
    route_weights,
    gate_saved,
    up_saved,
    gate_weight,
    up_weight,
    down_weight,
    queries,
    key_states,
    value_states,
    window_bias,
):
    lon_count = lax.axis_size("lon")
    lat_count = lax.axis_size("lat")
    section_count = lax.axis_size("section")
    windows = residual_stream.shape[2]
    points = residual_stream.shape[3]
    width = residual_stream.shape[4]
    tok_rows = windows * points
    capacity = gate_saved.shape[4]
    shard_width = gate_saved.shape[5]
    upstream = grad_out.reshape(tok_rows, width)
    lon = lax.axis_index("lon")
    x_place, corner = lon // 4, lax.rem(lon, 4)

    def swapped(x, bit):
        return lax.ppermute(x, "lon", [(i, i ^ bit) for i in range(lon_count)])

    def along_x(x, by):
        return lax.ppermute(x, "lon", [(i, (i + 4 * by) % lon_count) for i in range(lon_count)])

    across = swapped(upstream, 2)
    facts = jnp.concatenate(
        [
            expert_ids.reshape(tok_rows, TOP).T.astype(jnp.float32),
            route_weights.reshape(tok_rows, TOP).T,
            jnp.full((1, tok_rows), corner.astype(jnp.float32)),
        ],
        axis=0,
    )
    facts_across = swapped(facts, 2)
    core = swapped(upstream, 1)
    facts_core = swapped(facts, 1)
    facts_both = swapped(facts_across, 1)
    both = swapped(across, 1)
    slots = capacity + 1
    steps = (0, 1, -1, 2)
    row = jnp.arange(4 * slots, dtype=jnp.int32)
    row_codes = jnp.concatenate(
        [
            ((lax.rem(x_place + step + 4, 4) * 4 + corner) * 32 + row // 4) * 4 + row % 4
            for step in steps
        ]
    ).astype(jnp.float32)
    codes, *blocks = select_rows(
        row_codes.reshape(16 * slots, 1),
        (facts, facts_core, facts_across, facts_both),
        (upstream, core, across, both),
        (4 * slots,) * 4,
    )
    blocks = [blocks[0]] + [along_x(blocks[at], steps[at]) for at in (1, 2, 3)]
    combine = (
        (codes.reshape(4, TOP, tok_rows, 1) == row_codes)
        .any(axis=1)
        .reshape(4 * tok_rows, 16 * slots)
        .astype(jnp.bfloat16)
    )
    came = jnp.concatenate(
        [row // 4 * 16 + lax.rem(x_place - step + 4, 4) * 4 + row % 4 for step in steps]
    )
    places = jnp.arange(lon_count * capacity, dtype=jnp.int32)
    place = (places[:, None] == came[None, :]).astype(jnp.bfloat16)
    first = FIRST_SLOTS * lon_count
    arrived, high, low = placed_rows(
        place, blocks, (lon_count * capacity, first, lon_count * capacity - first)
    )
    gate_mat = gate_weight[0]
    up_mat = up_weight[0]
    down_mat = down_weight[0]
    gate_flat = gate_saved[0].transpose(0, 1, 3, 2, 4).reshape(
        lat_count, section_count, lon_count * capacity, shard_width
    )
    up_flat = up_saved[0].transpose(0, 1, 3, 2, 4).reshape(
        lat_count, section_count, lon_count * capacity, shard_width
    )
    lat = lax.axis_index("lat")
    section = lax.axis_index("section")

    def term(incoming, lat_step, section_step, low, high):
        at = (lax.rem(lat - lat_step + lat_count, lat_count), section ^ section_step, low, 0)
        size = (1, 1, high - low, shard_width)
        gate_rows = lax.dynamic_slice(gate_flat, at, size)[0, 0]
        up_rows = lax.dynamic_slice(up_flat, at, size)[0, 0]
        return expert_term(incoming, gate_rows, up_rows, gate_mat, up_mat, down_mat)

    count = lon_count * capacity
    half = count // 2
    half_high = first // 2
    landed = []

    def start(x, way):
        if landed:
            x = lax.optimization_barrier((x,) + tuple(landed))[0]
        if way:
            return passed_along(x, "lat", way)
        return passed_along(x, "section", 1)

    def both_ways(up, down):
        return start(up, 1), start(down, -1)

    def land(*arrays):
        landed.extend(arrays)
        del landed[:-8]

    def rounded(x):
        return x.astype(jnp.bfloat16)

    def widened(x):
        return x.astype(jnp.float32)

    def low_term(rows, step, side):
        return term(rows, step, side, first, count)

    def high_term(rows, step, side):
        return term(rows, step, side, 0, first)

    def far_back(x, cut):
        x = rounded(x)
        return both_ways(x[cut:], x[:cut])

    def near_back(up, down, got, cut):
        from_down, from_up = got
        up = jnp.concatenate([up[:cut] + widened(from_up), up[cut:]], axis=0)
        down = jnp.concatenate([down[:cut], down[cut:] + widened(from_down)], axis=0)
        return both_ways(rounded(down), rounded(up))

    def summed_up(own, got):
        return own + widened(got[0]) + widened(got[1])

    def held(x, *arrays):
        return lax.optimization_barrier((x,) + arrays)[0]

    up, down = both_ways(arrived, arrived)
    high_z = start(high, 0)
    own = jnp.concatenate([high_term(high, 0, 0), low_term(low, 0, 0)], axis=0)
    land(high_z, own)
    low_z = start(low, 0)
    query = queries.reshape(points, width)
    key = key_states.reshape(points, width)
    probs = probabilities(held(query, high_z), key, window_bias[0])
    t_high_z = high_term(high_z, 0, 1)
    land(up, down, probs, t_high_z)
    far = both_ways(up[:half], down[half:])
    land(low_z)
    low_up_z = start(up[first:], 0)
    t_up = (high_term(up[:first], 1, 0), low_term(up[first:], 1, 0))
    land(low_up_z, *t_up)
    low_down_z = start(down[first:], 0)
    high_up_z, high_down_z = both_ways(high_z, high_z)
    later = held(down, low_up_z)
    t_down = (high_term(later[:first], -1, 0), low_term(later[first:], -1, 0))
    t_low_z = low_term(held(low_z, low_up_z), 0, 1)
    land(*far, *t_down, t_low_z, low_down_z)
    far = jnp.concatenate(far, axis=0)
    low_far_z = start(far[first:], 0)
    later = held(far, low_down_z)
    t_far = (high_term(later[:first], 2, 0), low_term(later[first:], 2, 0))
    t_low_up_z = low_term(held(low_up_z, low_down_z), 1, 1)
    land(high_up_z, high_down_z, *t_far, t_low_up_z)
    far_z = both_ways(high_up_z[:half_high], high_down_z[half_high:])
    high_far_z = jnp.concatenate(far_z, axis=0)
    land(low_far_z)
    crossed_far = rounded(low_term(low_far_z, 2, 1))
    high_far_z = held(high_far_z, crossed_far)
    crossed_far = start(crossed_far, 0)
    far_1 = rounded(high_term(high_far_z, 2, 1))
    land(*far_z)
    far_1 = both_ways(far_1[half_high:], far_1[:half_high])
    t_up_z = high_term(held(high_up_z, crossed_far), 1, 1)
    t_down_z = high_term(held(high_down_z, crossed_far), -1, 1)
    t_low_down_z = low_term(held(low_down_z, crossed_far), -1, 1)
    land(*far_1)
    land(crossed_far)
    near_1 = near_back(t_up_z, t_down_z, far_1, half_high)
    land(crossed_far)
    crossed_up = start(rounded(t_low_up_z), 0)
    far_0 = far_back(
        jnp.concatenate(
            [
                t_far[0],
                t_far[1] + widened(crossed_far),
            ],
            axis=0,
        ),
        half,
    )
    land(crossed_up)
    crossed_down = start(rounded(t_low_down_z), 0)
    land(*near_1)
    land(*far_0)
    land(crossed_down)
    near_0 = near_back(
        jnp.concatenate(
            [
                t_up[0],
                t_up[1] + widened(crossed_up),
            ],
            axis=0,
        ),
        jnp.concatenate(
            [
                t_down[0],
                t_down[1] + widened(crossed_down),
            ],
            axis=0,
        ),
        far_0,
        half,
    )
    crossed_high = start(rounded(summed_up(t_high_z, near_1)), 0)
    land(crossed_high)
    crossed_low = start(rounded(t_low_z), 0)
    crossed = jnp.concatenate([crossed_high, crossed_low], axis=0)
    summed = rounded(summed_up(own + widened(crossed), near_0))
    returned = split_rows((came[:, None] == places[None, :]).astype(jnp.bfloat16), summed)
    returned = [returned[0]] + [along_x(returned[at], -steps[at]) for at in (1, 2, 3)]
    own_sum, across_sum, core_sum = combine_rows(combine, returned)
    core_sum = swapped(core_sum, 1)
    across_sum = rounded(across_sum + widened(core_sum[tok_rows:]))
    across_sum = swapped(across_sum, 2)
    grad_hidden, west = norm_grads(
        own_sum,
        core_sum,
        across_sum,
        residual_stream.reshape(points, width),
        upstream,
        norm_gain,
    )
    west = passed_along(west, "lon", -1)
    grad_queries, grad_keys, grad_values = attention_grads(
        grad_hidden, west, query, key, value_states.reshape(points, width), probs
    )
    out_shape = residual_stream.shape
    return (
        grad_hidden.reshape(out_shape),
        grad_queries.reshape(out_shape),
        grad_keys.reshape(out_shape),
        grad_values.reshape(out_shape),
    )


def solution(mesh):
    placed = (
        P("section", "lat", "lon", None, None),
        P("section", "lat", "lon", None, None),
        P(),
        P("section", "lat", "lon", None, None),
        P("section", "lat", "lon", None, None),
        P("lon", None, None, None, None, ("lat", "section")),
        P("lon", None, None, None, None, ("lat", "section")),
        P("lon", None, ("lat", "section")),
        P("lon", None, ("lat", "section")),
        P("lon", ("lat", "section"), None),
        P("section", "lat", "lon", None, None),
        P("section", "lat", "lon", None, None),
        P("section", "lat", "lon", None, None),
        P("lat", None, None, None),
    )
    return jax.shard_map(
        per_device,
        mesh=mesh,
        in_specs=placed,
        out_specs=(
            P("section", "lat", "lon", None, None),
            P("section", "lat", "lon", None, None),
            P("section", "lat", "lon", None, None),
            P("section", "lat", "lon", None, None),
        ),
        check_vma=False,
    )
```
